32 devices in a mesh: groups: 2 (over x), ctx: 16 (over z, y, core).
Axes of the slice: x: 2, y: 2, z: 4, core: 2. Of those that a mesh axis runs over, the one named last changes fastest.
Arguments:
- tokens: bfloat16 [3072, 1152], P(('groups', 'ctx')), parts along dimension 0, may hold values from -100 to 100
- owner: int32 [3072, 1], P(('groups', 'ctx')), parts along dimension 0, may hold values from 0 to 15; in each aligned block of 96 rows (0 to 95, 96 to 191, ...) at most 12 rows name the same one
- slot_map: int32 [32, 16, 12], P(('groups', 'ctx')), parts along dimension 0, may hold values from 0 to 47
- sizes: int32 [3072], P(('groups', 'ctx')), parts along dimension 0, may hold values from 1 to 4
- w_query: bfloat16 [1152, 576], replicated, may hold values from -0.1875 to 0.1875
- w_key: bfloat16 [1152, 576], replicated, may hold values from -0.1875 to 0.1875
- w_value: bfloat16 [1152, 576], replicated, may hold values from -0.1875 to 0.1875
- w_out: bfloat16 [576, 1152], replicated, may hold values from -0.25 to 0.25
Outputs:
- mixed: bfloat16 [3072, 1152], P(('groups', 'ctx')), parts along dimension 0
The draws below stay inside these ranges and needn't reach their ends.
There are 2 independent parts, one for each index of `groups`. The reference program is written for one: setup_inputs(seed, part) draws one part's arguments, and reference() takes and returns one part's arrays. A program takes and returns all parts, laid end to end along the dimension named above; an argument that names none is the same for every part. Nothing has to cross between parts.
Inputs may be any that keep to these rules, and one draw needn't show every extreme that they name: Among the source tokens of one index of ctx, at most 12 name the same owner, and in some index exactly 12 do.
All inputs are finite; a program needn't handle non-finite values.
Results may differ from the reference program's by a relative error of at most 0.0085.
The reference program's roundings to bfloat16 on the way (of `merged`, `key_bias`, `attended` and `merged_out`) count: a program that leaves them out, or rounds other values in their place, can miss the bound.
Values may be sent and summed in bfloat16 or wider, within the bound.
No kernel may reach another device: no remote copies, remote signals or barrier semaphores. Data moves between devices by JAX's collectives and lax.ppermute only.
A program may use at most 128 MiB of HBM per device.

```python
import math
import jax
import jax.numpy as jnp
import numpy as np
from jax import lax

D = 1152
HEADS = 8
HEAD = 72
TOK_DEV = 96
MDEV = 48
SHARDS = 16
SLOT = 12
TOKENS = 1536
MTOT = 768


def draw_tokens(key, part):
    base = jax.random.normal(key, (TOKENS, D), jnp.float32)
    base = jnp.clip(base, -6.0, 6.0)
    return base.astype(jnp.bfloat16)


def set_ends(values, rng, low, largest):
    longest = values.shape.index(max(values.shape))
    spots = []
    for shift in (0, 1):
        where = [jax.random.randint(jax.random.fold_in(rng, axis), (), 0, length) for axis, length in enumerate(values.shape)]
        where[longest] = (where[longest] + shift) % values.shape[longest]
        spots.append(tuple(where))
    return values.at[spots[0]].set(low).at[spots[1]].set(largest)


def assign_block(stream_key, own, number, rows, number_of, top, bound, lean):
    order = jax.random.permutation(stream_key, number_of)
    packed, ordinary = shares(number_of, rows * top, bound, lean, True), shares(number_of, rows * top, bound, lean, False)
    places = jnp.arange(number_of)

    def named(tallies, rotation):
        used = int((tallies > 0).sum())
        fixed = max(1, used // 4)
        moved = fixed + (places - fixed + rotation * (used - fixed)) % max(1, number_of - fixed)
        return jnp.zeros((number_of,), jnp.int32).at[order[jnp.where(places < fixed, places, moved)]].set(jnp.asarray(tallies, jnp.int32))

    tallies = jnp.where(number % 4 == 0, named(packed, number // 4), named(ordinary, number - number // 4 - 1))
    mixed = jax.random.permutation(jax.random.fold_in(own, 3), number_of)
    donor, receiver = mixed[0:number_of // 2 * 2:2], mixed[1:number_of // 2 * 2:2]
    room = jnp.minimum(tallies[donor] - 1, bound - tallies[receiver]) // 2
    room = jnp.where((donor == order[0]) | (receiver == order[0]) | (tallies[receiver] == 0), 0, jnp.maximum(room, 0))
    moved = jax.random.randint(jax.random.fold_in(own, 4), (number_of // 2,), 0, 1 << 20) % (room + 1)
    tallies = tallies.at[donor].add(-moved).at[receiver].add(moved)
    labels = jnp.searchsorted(jnp.cumsum(tallies), jnp.arange(rows * top), side="right").astype(jnp.int32)
    grid = labels.reshape(top, rows).T
    grid = grid[jax.random.permutation(jax.random.fold_in(own, 1), rows)]
    rotation = jax.random.randint(jax.random.fold_in(own, 2), (rows, 1), 0, top)
    return jnp.take_along_axis(grid, (jnp.arange(top)[None, :] + rotation) % top, axis=1)


def shares(count, total, bound, slope, full):
    portions = [(1 << 20) // math.isqrt(standing ** slope) + 1 for standing in range(1, count + 1)]
    largest = bound if full else min(bound, max(-(-total // count), total * portions[0] // sum(portions)))
    least = 1 if total - largest >= count - 1 else 0
    given, surplus = [largest] + [least] * (count - 1), total - largest - least * (count - 1)
    while surplus > 0:
        candidates = [i for i in range(1, count) if given[i] < largest] or [i for i in range(1, count) if given[i] < bound]
        mass, budget = sum([portions[i] for i in candidates]), surplus
        for i in candidates:
            more = min(bound - given[i], max(1, budget * portions[i] // mass), surplus)
            given[i] = given[i] + more
            surplus = surplus - more
    return np.array(given)


def scatter_about(rng, dims, scale, most, held_as=jnp.bfloat16):
    values = jax.random.normal(rng, dims, jnp.float32) * scale
    return jnp.minimum(jnp.maximum(values, -most), most).astype(held_as)


def setup_inputs(seed: int = 0, part: int = 0) -> dict:
    seeds = jax.random.split(jax.random.key(seed), 9)
    part_splits = jax.random.split(jax.random.fold_in(seeds[8], part), 9)
    tokens = draw_tokens(jax.random.fold_in(jax.random.fold_in(seeds[8], part), 71), part)
    owner_keys = jax.random.split(jax.random.fold_in(part_splits[1], 1), TOKENS // TOK_DEV)
    owner_turns = jax.random.permutation(jax.random.fold_in(part_splits[1], 3), TOKENS // TOK_DEV)
    owner = jax.vmap(lambda own, number: assign_block(jax.random.fold_in(part_splits[1], 2), own, number, TOK_DEV, SHARDS, 1, SLOT, 2))(owner_keys, owner_turns).reshape((TOKENS, 1))
    slot_map = set_ends(jax.random.randint(part_splits[2], (SHARDS, SHARDS, SLOT), 0, MDEV), jax.random.fold_in(part_splits[2], 1), 0, MDEV - 1).astype(jnp.int32)
    sizes = set_ends(jax.random.randint(part_splits[3], (TOKENS,), 1, 5), jax.random.fold_in(part_splits[3], 1), 1, 4).astype(jnp.int32)
    w_query = scatter_about(seeds[4], (D, HEADS * HEAD), D ** -0.5, 0.1875)
    w_key = scatter_about(seeds[5], (D, HEADS * HEAD), D ** -0.5, 0.1875)
    w_value = scatter_about(seeds[6], (D, HEADS * HEAD), D ** -0.5, 0.1875)
    w_out = scatter_about(seeds[7], (HEADS * HEAD, D), (HEADS * HEAD) ** -0.5, 0.25)
    return dict(tokens=tokens, owner=owner, slot_map=slot_map, sizes=sizes, w_query=w_query, w_key=w_key, w_value=w_value, w_out=w_out)


def reference(tokens, owner, slot_map, sizes, w_query, w_key, w_value, w_out):
    owners = owner[:, 0].reshape(SHARDS, TOK_DEV).astype(jnp.int32)
    marks = (owners[:, :, None] == jnp.arange(SHARDS, dtype=jnp.int32)[None, None, :]).astype(jnp.int32)
    ranking = lax.optimization_barrier(jnp.sum((jnp.cumsum(marks, axis=1) - marks) * marks, axis=2)).astype(jnp.int32)
    senders = jnp.broadcast_to(jnp.arange(SHARDS, dtype=jnp.int32)[:, None], (SHARDS, TOK_DEV))
    dest = (owners * MDEV + slot_map[owners, senders, ranking]).reshape(TOKENS).astype(jnp.int32)
    weights = sizes.astype(jnp.float32)
    counts = jax.ops.segment_sum(weights, dest, num_segments=MTOT)
    merged_sum = jax.ops.segment_sum(weights[:, None] * tokens.astype(jnp.float32), dest, num_segments=MTOT)
    merged = (merged_sum / jnp.maximum(counts, 1.0)[:, None]).astype(jnp.bfloat16)
    bias_low = jnp.where(counts > 0, jnp.log(jnp.maximum(counts, 1.0)), -1e+30).astype(jnp.bfloat16)
    key_bias = lax.optimization_barrier(bias_low).astype(jnp.float32)
    queries = jnp.dot(merged, w_query, preferred_element_type=jnp.float32).astype(jnp.bfloat16)
    keys = jnp.dot(merged, w_key, preferred_element_type=jnp.float32).astype(jnp.bfloat16)
    values = jnp.dot(merged, w_value, preferred_element_type=jnp.float32).astype(jnp.bfloat16)
    key_heads = keys.reshape(MTOT, HEADS, HEAD).astype(jnp.float32)
    value_heads = values.reshape(MTOT, HEADS, HEAD).astype(jnp.float32)
    inverse = 1.0 / math.sqrt(HEAD)
    block = math.gcd(MTOT, 512)

    def block_attend(query_block):
        scores = jnp.einsum('qhd,khd->hqk', query_block.astype(jnp.float32), key_heads) * inverse
        scores = scores + key_bias[None, None, :]
        top = lax.optimization_barrier(jnp.max(scores, axis=2, keepdims=True))
        expo = jnp.exp(scores - top)
        total = lax.optimization_barrier(jnp.sum(expo, axis=2))
        rounded = lax.optimization_barrier(expo.astype(jnp.bfloat16)).astype(jnp.float32)
        accum = jnp.einsum('hqk,khd->hqd', rounded, value_heads)
        result = accum / total[:, :, None]
        return jnp.transpose(result, (1, 0, 2)).reshape(block, HEADS * HEAD).astype(jnp.bfloat16)
    attended = lax.map(block_attend, queries.reshape(MTOT // block, block, HEADS, HEAD))
    attended = attended.reshape(MTOT, HEADS * HEAD)
    merged_out = jnp.dot(attended, w_out, preferred_element_type=jnp.float32).astype(jnp.bfloat16)
    return merged_out[dest]
```

```python
import functools
import math

import jax
import jax.numpy as jnp
from jax import lax
from jax.experimental import pallas as pl
from jax.experimental.pallas import tpu as pltpu
from jax.sharding import PartitionSpec as P

HEADS = 8
HEAD = 72
META = 16
LANES = 128
GATHERED_MAX = 8 << 20
VMEM_PREP = 16 << 20
VMEM_TAIL = 44 << 20
F32 = jnp.float32
BF16 = jnp.bfloat16
NT = (((1,), (1,)), ((), ()))
TN = (((0,), (0,)), ((), ()))
NN = (((1,), (0,)), ((), ()))


def dot(a, b, dims=NN):
    return lax.dot_general(a, b, dims, preferred_element_type=F32)


def ring_index(k, core, rows):
    k = k % (2 * rows)
    row, column = (k, 0) if k < rows else (2 * rows - 1 - k, 1)
    return row * 4 + column * 2 + core


def ring_moves(shards):
    rows = shards // 4
    moves = []
    for k in range(2 * rows):
        for core, step in ((0, 1), (1, -1)):
            moves.append((ring_index(k, core, rows), ring_index(k + step, core, rows)))
    return moves


def sender_table(shards):
    rows = shards // 4
    position = {ring_index(k, c, rows): (k, c) for k in range(2 * rows) for c in (0, 1)}
    table = []
    for me in range(shards):
        k, c = position[me]
        d = -1 if c == 0 else 1
        row = [me, me ^ 1]
        for s in range(1, rows):
            row += [
                ring_index(k + d * s, c, rows),
                ring_index(k + d * s, c ^ 1, rows),
                ring_index(k - d * s, c ^ 1, rows),
                ring_index(k - d * s, c, rows),
            ]
        row += [ring_index(k + d * rows, c, rows), ring_index(k - d * rows, c ^ 1, rows)]
        table.append(row)
    return table


def meta_kernel(slots, owner_col_ref, owner_row_ref, sizes_ref, map_ref, out_ref):
    tok = owner_row_ref.shape[1]
    row = owner_row_ref[...]
    earlier = lax.broadcasted_iota(jnp.int32, (tok, tok), 0) < lax.broadcasted_iota(
        jnp.int32, (tok, tok), 1
    )
    same = jnp.where(owner_col_ref[...] == row, 1, 0)
    rank = jnp.sum(jnp.where(earlier, same, 0), axis=0, keepdims=True)
    sub = lax.broadcasted_iota(jnp.int32, (META, LANES), 0)

    def wide(x, rows):
        x = x.astype(F32)
        x = jnp.concatenate([x, jnp.zeros((x.shape[0], LANES - x.shape[1]), F32)], axis=1)
        if x.shape[0] == 1:
            return jnp.broadcast_to(x, (META, LANES))
        return jnp.concatenate([x, jnp.zeros((META - rows, LANES), F32)], axis=0)

    out = wide(map_ref[...], slots)
    out = jnp.where(sub == slots, wide(row, 1), out)
    out = jnp.where(sub == slots + 1, wide(rank, 1), out)
    out = jnp.where(sub == slots + 2, wide(sizes_ref[...], 1), out)
    out_ref[...] = out.astype(BF16)


def prep_kernel(
    shards, slots, tok, merged_rows, me_ref, table_ref, g_ref,
    m_ref, inv_ref, bias_ref, pick_ref, gf, dest_row, size_row,
):
    me = me_ref[0]
    total = merged_rows * shards
    gf[...] = g_ref[...].astype(F32)
    by_sender = jnp.transpose(gf[...], (1, 0))[:shards].astype(BF16)
    places = shards * META
    bucket = lax.broadcasted_iota(jnp.int32, (places, LANES), 0)
    sender_iota = lax.broadcasted_iota(jnp.int32, (shards, LANES), 0)
    for j in range(shards):
        e = table_ref[j]
        base = (e ^ me) * META
        own = gf[pl.ds(base + slots, 1), :].astype(jnp.int32)
        rank = gf[pl.ds(base + slots + 1, 1), :].astype(jnp.int32)
        size = gf[pl.ds(base + slots + 2, 1), :]
        hot = jnp.where(bucket == (own ^ me) * META + rank, 1.0, 0.0).astype(BF16)
        found = dot(by_sender, hot)
        slot = jnp.sum(jnp.where(sender_iota == e, found, 0.0), axis=0, keepdims=True)
        dest = own.astype(F32) * merged_rows + slot
        dest_row[:, j * tok : (j + 1) * tok] = dest[:, :tok]
        size_row[:, j * tok : (j + 1) * tok] = size[:, :tok]
    places_iota = lax.broadcasted_iota(jnp.int32, (total, LANES), 0).astype(F32)
    count = jnp.zeros((total, LANES), F32)
    for b in range(shards * tok // LANES):
        cols = slice(b * LANES, (b + 1) * LANES)
        piece = jnp.where(places_iota == dest_row[:, cols], size_row[:, cols], 0.0)
        count = count + piece
        m_ref[:, cols] = piece.astype(BF16)
    inv_ref[...] = 1.0 / jnp.maximum(jnp.sum(count, axis=1, keepdims=True), 1.0)
    count_row = dot(jnp.ones((8, LANES), BF16), count.astype(BF16), NT)[0:1]
    bias = jnp.where(count_row > 0, jnp.log(jnp.maximum(count_row, 1.0)), -1e30)
    bias_ref[...] = bias.astype(BF16).astype(F32)
    mine = jnp.broadcast_to(dest_row[:, :LANES], (8, LANES))
    mine = jnp.transpose(mine, (1, 0))[:tok, 0:1]
    lane = lax.broadcasted_iota(jnp.int32, (tok, total), 1).astype(F32)
    pick_ref[...] = jnp.where(lane == mine, 1.0, 0.0).astype(BF16)


def tail_kernel(n_blocks, *refs):
    blocks = refs[:n_blocks]
    (m_ref, inv_ref, bias_ref, pick_ref, wq_ref, wk_ref, wv_ref, wo_ref, out_ref,
     tok_s, merged_s, att_s) = refs[n_blocks:]
    tok = blocks[0].shape[0]
    for j in range(n_blocks):
        tok_s[j * tok : (j + 1) * tok, :] = blocks[j][...]
    total = m_ref.shape[0]
    tile = 256

    def merge(i, _):
        rows = pl.ds(pl.multiple_of(i * tile, tile), tile)
        acc = dot(m_ref[rows, :], tok_s[...])
        merged_s[rows, :] = (acc * inv_ref[rows, :]).astype(BF16)
        return 0

    lax.fori_loop(0, total // tile, merge, 0)
    merged = merged_s[...]
    picked = dot(pick_ref[...], merged).astype(BF16)
    q_t = dot(wq_ref[...], picked, NT).astype(BF16)
    inverse = 1.0 / math.sqrt(HEAD)
    bias = bias_ref[...]
    k_t = dot(wk_ref[...], merged, NT)
    v_t = dot(wv_ref[...], merged, NT)
    for h in range(HEADS):
        rows = slice(h * HEAD, (h + 1) * HEAD)
        q_h = q_t[rows].astype(BF16)
        scores = dot(q_h, k_t[rows].astype(BF16), TN) * inverse + bias
        top = jnp.max(scores, axis=1, keepdims=True)
        expo = jnp.exp(scores - top)
        whole = jnp.sum(expo, axis=1, keepdims=True)
        att = dot(expo.astype(BF16), v_t[rows].astype(BF16), NT) / whole
        att_s[:, rows] = att
    out_ref[...] = dot(att_s[...].astype(BF16), wo_ref[...]).astype(BF16)


def on_device_gathered(tokens, owner, slot_map, sizes, w_query, w_key, w_value, w_out):
    tok, width = tokens.shape
    shards = lax.axis_size("ctx")
    slots = slot_map.shape[2]
    merged_rows = tok // 2
    total = merged_rows * shards
    vmem = pl.BlockSpec(memory_space=pltpu.VMEM)
    smem = pl.BlockSpec(memory_space=pltpu.SMEM)
    me = lax.axis_index("ctx")
    moves = ring_moves(shards)
    swap = [(i, i ^ 1) for i in range(shards)]

    def send(x, pairs):
        return lax.ppermute(x, "ctx", pairs)

    meta = pl.pallas_call(
        functools.partial(meta_kernel, slots),
        out_shape=jax.ShapeDtypeStruct((META, LANES), BF16),
        in_specs=[vmem] * 4,
        out_specs=vmem,
    )(owner, owner.reshape(1, tok), sizes.reshape(1, tok), jnp.transpose(slot_map[0], (1, 0)))
    bit = 1
    while bit < shards:
        meta = jnp.concatenate([meta, send(meta, [(i, i ^ bit) for i in range(shards)])], axis=0)
        bit *= 2

    other = send(tokens, swap)
    a, b = tokens, other
    blocks = [tokens, other]
    for s in range(1, shards // 4):
        a = send(a, moves)
        b = send(b, moves)
        blocks += [a, b, send(a, swap), send(b, swap)]
    a = send(a, moves)
    blocks += [a, send(a, swap)]

    table = jnp.array(sender_table(shards), jnp.int32)[me]
    m, inv, bias, pick = pl.pallas_call(
        functools.partial(prep_kernel, shards, slots, tok, merged_rows),
        out_shape=(
            jax.ShapeDtypeStruct((total, shards * tok), BF16),
            jax.ShapeDtypeStruct((total, 1), F32),
            jax.ShapeDtypeStruct((1, total), F32),
            jax.ShapeDtypeStruct((tok, total), BF16),
        ),
        in_specs=[smem, smem, vmem],
        out_specs=(vmem,) * 4,
        scratch_shapes=[
            pltpu.VMEM((shards * META, LANES), F32),
            pltpu.VMEM((1, shards * tok), F32),
            pltpu.VMEM((1, shards * tok), F32),
        ],
        compiler_params=pltpu.CompilerParams(vmem_limit_bytes=VMEM_PREP),
    )(me.reshape(1), table, meta)
    return pl.pallas_call(
        functools.partial(tail_kernel, len(blocks)),
        out_shape=jax.ShapeDtypeStruct((tok, width), BF16),
        in_specs=[vmem] * (len(blocks) + 8),
        out_specs=vmem,
        scratch_shapes=[
            pltpu.VMEM((shards * tok, width), BF16),
            pltpu.VMEM((total, width), BF16),
            pltpu.VMEM((tok, HEADS * HEAD), F32),
        ],
        compiler_params=pltpu.CompilerParams(vmem_limit_bytes=VMEM_TAIL),
    )(*blocks, m, inv, bias, pick, w_query.T, w_key.T, w_value.T, w_out)


def on_device_exchanged(tokens, owner, slot_map, sizes, w_query, w_key, w_value, w_out):
    tok_rows = tokens.shape[0]
    shards = lax.axis_size("ctx")
    slots = slot_map.shape[2]
    places = shards * slots
    merged_rows = tok_rows // 2
    owners = owner[:, 0]
    order = jnp.arange(tok_rows)
    earlier = order[None, :] < order[:, None]
    ranking = jnp.sum(jnp.where(earlier & (owners[:, None] == owners[None, :]), 1, 0), axis=1)
    bucket = owners * slots + ranking
    to_bucket = (bucket[:, None] == jnp.arange(places, dtype=jnp.int32)[None, :]).astype(
        jnp.bfloat16
    )
    outgoing = jnp.einsum(
        "tp,td->pd", to_bucket, tokens, preferred_element_type=jnp.float32
    ).astype(jnp.bfloat16)
    out_weights = jnp.einsum(
        "tp,t->p", to_bucket, sizes.astype(jnp.bfloat16), preferred_element_type=jnp.float32
    ).astype(jnp.bfloat16)
    received, in_weights = (
        lax.all_to_all(
            outgoing.reshape(shards, slots, -1), "ctx", split_axis=0, concat_axis=0, tiled=True
        ),
        lax.all_to_all(
            out_weights.reshape(shards, slots), "ctx", split_axis=0, concat_axis=0, tiled=True
        ),
    )
    targets = slot_map[0].reshape(places)
    landing = targets[None, :] == jnp.arange(merged_rows, dtype=jnp.int32)[:, None]
    weighted = jnp.where(landing, in_weights.reshape(places)[None, :], 0)
    merged_sum = jnp.dot(weighted, received.reshape(places, -1), preferred_element_type=jnp.float32)
    counts = jnp.sum(weighted.astype(jnp.float32), axis=1)
    merged = (merged_sum / jnp.maximum(counts, 1.0)[:, None]).astype(jnp.bfloat16)
    key_bias = jnp.where(counts > 0, jnp.log(jnp.maximum(counts, 1.0)), -1e30).astype(jnp.bfloat16)
    queries = jnp.dot(merged, w_query, preferred_element_type=jnp.float32).astype(jnp.bfloat16)
    query_heads = queries.reshape(merged_rows, HEADS, HEAD)
    inverse = 1.0 / math.sqrt(HEAD)

    def attend_block(carry, item):
        row_max, total, accum = carry
        key_heads, value_heads, bias = item
        scores = (
            jnp.einsum("qhd,khd->hqk", query_heads, key_heads, preferred_element_type=jnp.float32)
            * inverse
        )
        scores = scores + bias.astype(jnp.float32)[None, None, :]
        new_max = jnp.maximum(row_max, jnp.max(scores, axis=2))
        factor = jnp.exp(row_max - new_max)
        expo = jnp.exp(scores - new_max[:, :, None])
        total = total * factor + jnp.sum(expo, axis=2)
        accum = accum * factor[:, :, None] + jnp.einsum(
            "hqk,khd->hqd",
            expo.astype(jnp.bfloat16),
            value_heads,
            preferred_element_type=jnp.float32,
        )
        return ((new_max, total, accum), None)

    start_state = (
        jnp.full((HEADS, merged_rows), -jnp.inf, jnp.float32),
        jnp.zeros((HEADS, merged_rows), jnp.float32),
        jnp.zeros((HEADS, merged_rows, HEAD), jnp.float32),
    )
    own_keys = jnp.dot(merged, w_key, preferred_element_type=jnp.float32).astype(jnp.bfloat16)
    own_values = jnp.dot(merged, w_value, preferred_element_type=jnp.float32).astype(jnp.bfloat16)
    carry = start_state
    keys = lax.all_gather(own_keys, "ctx", axis=0, tiled=True)
    values = lax.all_gather(own_values, "ctx", axis=0, tiled=True)
    bias = lax.all_gather(key_bias, "ctx", axis=0, tiled=True)
    length = keys.shape[0]
    block = math.gcd(length, 1536)
    turns = length // block
    items = (
        keys.reshape(turns, block, HEADS, HEAD),
        values.reshape(turns, block, HEADS, HEAD),
        bias.reshape(turns, block),
    )
    carry, unused = lax.scan(attend_block, carry, items)
    row_max, total, accum = carry
    attended = (
        jnp.transpose(accum / total[:, :, None], (1, 0, 2))
        .reshape(merged_rows, HEADS * HEAD)
        .astype(jnp.bfloat16)
    )
    landing_rows = landing.astype(jnp.bfloat16)
    leaving = jnp.einsum(
        "mp,md->pd", landing_rows, attended, preferred_element_type=jnp.float32
    ).astype(jnp.bfloat16)
    returned = lax.all_to_all(
        leaving.reshape(shards, slots, -1), "ctx", split_axis=0, concat_axis=0, tiled=True
    )
    picked = jnp.einsum(
        "tp,pd->td", to_bucket, returned.reshape(places, -1), preferred_element_type=jnp.float32
    ).astype(jnp.bfloat16)
    mixed = jnp.dot(picked, w_out, preferred_element_type=jnp.float32).astype(jnp.bfloat16)
    return mixed


def on_device(tokens, owner, slot_map, *weights):
    tok, width = tokens.shape
    shards = lax.axis_size("ctx")
    fits = shards * tok * width * tokens.dtype.itemsize <= GATHERED_MAX
    paired = shards >= 8 and shards & (shards - 1) == 0 and shards <= LANES
    shaped = slot_map.shape[2] + 3 <= META and tok <= LANES and (shards * tok) % LANES == 0
    plan = on_device_gathered if fits and paired and shaped else on_device_exchanged
    return plan(tokens, owner, slot_map, *weights)


def solution(mesh):
    in_specs = (
        P(("groups", "ctx"), None),
        P(("groups", "ctx"), None),
        P(("groups", "ctx"), None, None),
        P(("groups", "ctx")),
        P(),
        P(),
        P(),
        P(),
    )
    out_specs = P(("groups", "ctx"), None)
    return jax.shard_map(
        on_device, mesh=mesh, in_specs=in_specs, out_specs=out_specs, check_vma=False
    )
```

```python
import functools
import math

import jax
import jax.numpy as jnp
from jax import lax
from jax.experimental import pallas as pl
from jax.experimental.pallas import tpu as pltpu
from jax.sharding import PartitionSpec as P

HEADS = 8
HEAD = 72
META = 16
LANES = 128
GATHERED_MAX = 8 << 20
VMEM_PREP = 16 << 20
VMEM_MERGE = 12 << 20
VMEM_TAIL = 20 << 20
F32 = jnp.float32
BF16 = jnp.bfloat16
NT = (((1,), (1,)), ((), ()))
TN = (((0,), (0,)), ((), ()))
NN = (((1,), (0,)), ((), ()))


def dot(a, b, dims=NN):
    return lax.dot_general(a, b, dims, preferred_element_type=F32)


def ring_index(k, core, rows):
    k = k % (2 * rows)
    row, column = (k, 0) if k < rows else (2 * rows - 1 - k, 1)
    return row * 4 + column * 2 + core


def ring_moves(shards, crossing):
    rows = shards // 4
    moves = []
    for k in range(2 * rows):
        for core, step in ((0, 1), (1, -1)):
            source = ring_index(k, core ^ crossing, rows)
            moves.append((source, ring_index(k + step, core, rows)))
    return moves


def senders(shards, me):
    rows = shards // 4
    row, column, core = me // 4, (me // 2) % 2, me % 2
    k = jnp.where(column == 0, row, 2 * rows - 1 - row)
    d = 2 * core - 1

    def at(offset, core):
        p = (k + offset + 2 * rows) % (2 * rows)
        back = p >= rows
        row = jnp.where(back, 2 * rows - 1 - p, p)
        return row * 4 + jnp.where(back, 2, 0) + core

    swapped = 1 - core
    found = [me, me ^ 1]
    for s in range(1, rows):
        found += [at(d * s, core), at(-d * s, swapped), at(d * s, swapped), at(-d * s, core)]
    return found + [at(d * rows, core), at(-d * rows, swapped)]


def flip(x, shards):
    return x % 2 * (shards // 2) + x // 2 % 2 * (shards // 4) + x // 4


def meta_kernel(slots, owner_ref, sizes_ref, map_ref, out_ref):
    tok = owner_ref.shape[1]

    def wide(x):
        x = x.astype(F32)
        return jnp.concatenate([x, jnp.zeros((1, LANES - x.shape[1]), F32)], axis=1)

    row = wide(owner_ref[...])
    column = jnp.transpose(jnp.broadcast_to(row, (8, LANES)), (1, 0))[:, 0:1]
    first = lax.broadcasted_iota(jnp.int32, (LANES, LANES), 0)
    second = lax.broadcasted_iota(jnp.int32, (LANES, LANES), 1)
    earlier = (first < second) & (column == row)
    rank = jnp.sum(jnp.where(earlier, 1.0, 0.0), axis=0, keepdims=True)
    rows = [wide(map_ref[r]) for r in range(slots)] + [row, rank, wide(sizes_ref[...])]
    sub = lax.broadcasted_iota(jnp.int32, (META, LANES), 0)
    out = jnp.zeros((META, LANES), F32)
    for r, x in enumerate(rows):
        out = jnp.where(sub == r, x, out)
    out_ref[...] = out.astype(BF16)


def prep_kernel(
    shards, slots, tok, merged_rows, g_ref,
    m_ref, inv_ref, bias_ref, pick_ref, gf, dest_row, size_row,
):
    me = lax.axis_index("ctx")
    me_flipped = flip(me, shards)
    total = merged_rows * shards
    gf[...] = g_ref[...].astype(F32)
    by_sender = jnp.transpose(gf[...], (1, 0))[:shards].astype(BF16)
    places = shards * META
    bucket = lax.broadcasted_iota(jnp.int32, (places, LANES), 0)
    sender_iota = lax.broadcasted_iota(jnp.int32, (shards, LANES), 0)
    for j, e in enumerate(senders(shards, me)):
        base = flip(e ^ me, shards) * META
        own = gf[pl.ds(base + slots, 1), :].astype(jnp.int32)
        rank = gf[pl.ds(base + slots + 1, 1), :].astype(jnp.int32)
        size = gf[pl.ds(base + slots + 2, 1), :]
        hot = jnp.where(bucket == (flip(own, shards) ^ me_flipped) * META + rank, 1.0, 0.0).astype(BF16)
        found = dot(by_sender, hot)
        slot = jnp.sum(jnp.where(sender_iota == e, found, 0.0), axis=0, keepdims=True)
        dest = own.astype(F32) * merged_rows + slot
        dest_row[:, j * tok : (j + 1) * tok] = dest[:, :tok]
        size_row[:, j * tok : (j + 1) * tok] = size[:, :tok]
    places_iota = lax.broadcasted_iota(jnp.int32, (total, LANES), 0).astype(F32)
    count = jnp.zeros((total, LANES), F32)
    for b in range(shards * tok // LANES):
        cols = slice(b * LANES, (b + 1) * LANES)
        piece = jnp.where(places_iota == dest_row[:, cols], size_row[:, cols], 0.0)
        count = count + piece
        m_ref[:, cols] = piece.astype(BF16)
    inv_ref[...] = 1.0 / jnp.maximum(jnp.sum(count, axis=1, keepdims=True), 1.0)
    count_row = dot(jnp.ones((8, LANES), BF16), count.astype(BF16), NT)[0:1]
    bias = jnp.where(count_row > 0, jnp.log(jnp.maximum(count_row, 1.0)), -1e30)
    bias_ref[...] = bias.astype(BF16).astype(F32)
    mine = jnp.broadcast_to(dest_row[:, :LANES], (8, LANES))
    mine = jnp.transpose(mine, (1, 0))[:tok, 0:1]
    lane = lax.broadcasted_iota(jnp.int32, (tok, total), 1).astype(F32)
    pick_ref[...] = jnp.where(lane == mine, 1.0, 0.0).astype(BF16)


def cost(flops, nbytes):
    return pl.CostEstimate(flops=flops, bytes_accessed=nbytes, transcendentals=0)


def gather_blocks(blocks, tok_s):
    tok = blocks[0].shape[0]
    for j, block in enumerate(blocks):
        tok_s[j * tok : (j + 1) * tok, :] = block[...]


def merge_kernel(n_blocks, first, *refs):
    blocks, (m_ref, *before, acc_ref, tok_s) = refs[:n_blocks], refs[n_blocks:]
    gather_blocks(blocks, tok_s)
    cols = slice(first, first + tok_s.shape[0])
    acc = dot(m_ref[:, cols], tok_s[...])
    acc_ref[...] = acc + before[0][...] if before else acc


def tail_kernel(n_blocks, first, *refs):
    blocks = refs[:n_blocks]
    (acc_ref, m_ref, inv_ref, bias_ref, pick_ref, wq_ref, wk_ref, wv_ref, wo_ref, out_ref,
     tok_s, merged_s, att_s) = refs[n_blocks:]
    gather_blocks(blocks, tok_s)
    acc = acc_ref[...] + dot(m_ref[:, first:], tok_s[...])
    merged_s[...] = (acc * inv_ref[...]).astype(BF16)
    merged = merged_s[...]
    picked = dot(pick_ref[...], merged).astype(BF16)
    q_t = dot(wq_ref[...], picked, NT)
    inverse = 1.0 / math.sqrt(HEAD)
    bias = bias_ref[...]
    k_t = dot(wk_ref[...], merged, NT)
    v_t = dot(wv_ref[...], merged, NT)
    for h in range(HEADS):
        rows = slice(h * HEAD, (h + 1) * HEAD)
        scores = dot(q_t[rows].astype(BF16), k_t[rows].astype(BF16), TN) * inverse + bias
        top = jnp.max(scores, axis=1, keepdims=True)
        expo = jnp.exp(scores - top)
        whole = jnp.sum(expo, axis=1, keepdims=True)
        att_s[:, rows] = dot(expo.astype(BF16), v_t[rows].astype(BF16), NT) / whole
    out_ref[...] = dot(att_s[...].astype(BF16), wo_ref[...]).astype(BF16)


def on_device_gathered(tokens, owner, slot_map, sizes, w_query, w_key, w_value, w_out):
    tok, width = tokens.shape
    shards = lax.axis_size("ctx")
    slots = slot_map.shape[2]
    merged_rows = tok // 2
    total = merged_rows * shards
    vmem = pl.BlockSpec(memory_space=pltpu.VMEM)
    swap = [(i, i ^ 1) for i in range(shards)]
    along, across = ring_moves(shards, 0), ring_moves(shards, 1)

    def send(x, pairs, *after):
        if after:
            x, *_ = lax.optimization_barrier((x, *after))
        return lax.ppermute(x, "ctx", pairs)

    a, b = send(tokens, along), send(tokens, across)
    other = send(tokens, swap)
    meta = pl.pallas_call(
        functools.partial(meta_kernel, slots),
        out_shape=jax.ShapeDtypeStruct((META, LANES), BF16),
        in_specs=[vmem] * 3,
        out_specs=vmem,
    )(owner.reshape(1, tok), sizes.reshape(1, tok), jnp.transpose(slot_map, (2, 0, 1)))
    metas = [meta]
    bit = shards // 2

    def spread(*after):
        nonlocal bit
        if bit:
            pairs = [(i, i ^ bit) for i in range(shards)]
            metas.append(send(jnp.concatenate(metas, axis=0), pairs, *after))
            bit //= 2

    a1 = a
    def xor(x, d, *after):
        return send(x, [(i, i ^ d) for i in range(shards)], *after)

    row = jnp.concatenate([meta] + [xor(meta, d, *(other,)) for d in range(4, shards, 4)], axis=0)
    plane = jnp.concatenate([row, xor(row, 2)], axis=0)
    metas = [plane, xor(plane, 1)]
    blocks = [tokens, other]
    for s in range(1, shards // 4):
        blocks += [a, send(a, swap), b, send(b, swap)]
        a = send(a, along)
        if s < shards // 4 - 1:
            b = send(b, along)
    m, inv, bias, pick = pl.pallas_call(
        functools.partial(prep_kernel, shards, slots, tok, merged_rows),
        out_shape=(
            jax.ShapeDtypeStruct((total, shards * tok), BF16),
            jax.ShapeDtypeStruct((total, 1), F32),
            jax.ShapeDtypeStruct((1, total), F32),
            jax.ShapeDtypeStruct((tok, total), BF16),
        ),
        in_specs=[vmem],
        out_specs=(vmem,) * 4,
        scratch_shapes=[
            pltpu.VMEM((shards * META, LANES), F32),
            pltpu.VMEM((1, shards * tok), F32),
            pltpu.VMEM((1, shards * tok), F32),
        ],
        compiler_params=pltpu.CompilerParams(vmem_limit_bytes=VMEM_PREP),
    )(jnp.concatenate(metas, axis=0))
    cuts = [0, shards // 2, shards - 4, shards]
    acc = []
    for low, high in zip(cuts[:-2], cuts[1:-1]):
        n = high - low
        acc = [
            pl.pallas_call(
                functools.partial(merge_kernel, n, low * tok),
                out_shape=jax.ShapeDtypeStruct((total, width), F32),
                in_specs=[vmem] * (n + 1 + len(acc)),
                out_specs=vmem,
                scratch_shapes=[pltpu.VMEM((n * tok, width), BF16)],
                input_output_aliases={n + 1: 0} if acc else {},
                compiler_params=pltpu.CompilerParams(vmem_limit_bytes=VMEM_MERGE),
            )(*blocks[low:high], m, *acc)
        ]
    blocks += [a, send(a, swap, *acc)]
    low, high = cuts[-2:]
    n = high - low
    return pl.pallas_call(
        functools.partial(tail_kernel, n, low * tok),
        out_shape=jax.ShapeDtypeStruct((tok, width), BF16),
        in_specs=[vmem] * (n + 9),
        out_specs=vmem,
        scratch_shapes=[
            pltpu.VMEM((n * tok, width), BF16),
            pltpu.VMEM((total, width), BF16),
            pltpu.VMEM((tok, HEADS * HEAD), F32),
        ],
        compiler_params=pltpu.CompilerParams(vmem_limit_bytes=VMEM_TAIL),
        cost_estimate=cost(4 * total * width * HEADS * HEAD, 8 * width * HEADS * HEAD),
    )(*blocks[low:high], *acc, m, inv, bias, pick, w_query.T, w_key.T, w_value.T, w_out)


def on_device_exchanged(tokens, owner, slot_map, sizes, w_query, w_key, w_value, w_out):
    tok_rows = tokens.shape[0]
    shards = lax.axis_size("ctx")
    slots = slot_map.shape[2]
    places = shards * slots
    merged_rows = tok_rows // 2
    owners = owner[:, 0]
    order = jnp.arange(tok_rows)
    earlier = order[None, :] < order[:, None]
    ranking = jnp.sum(jnp.where(earlier & (owners[:, None] == owners[None, :]), 1, 0), axis=1)
    bucket = owners * slots + ranking
    to_bucket = (bucket[:, None] == jnp.arange(places, dtype=jnp.int32)[None, :]).astype(
        jnp.bfloat16
    )
    outgoing = jnp.einsum(
        "tp,td->pd", to_bucket, tokens, preferred_element_type=jnp.float32
    ).astype(jnp.bfloat16)
    out_weights = jnp.einsum(
        "tp,t->p", to_bucket, sizes.astype(jnp.bfloat16), preferred_element_type=jnp.float32
    ).astype(jnp.bfloat16)
    received, in_weights = (
        lax.all_to_all(
            outgoing.reshape(shards, slots, -1), "ctx", split_axis=0, concat_axis=0, tiled=True
        ),
        lax.all_to_all(
            out_weights.reshape(shards, slots), "ctx", split_axis=0, concat_axis=0, tiled=True
        ),
    )
    targets = slot_map[0].reshape(places)
    landing = targets[None, :] == jnp.arange(merged_rows, dtype=jnp.int32)[:, None]
    weighted = jnp.where(landing, in_weights.reshape(places)[None, :], 0)
    merged_sum = jnp.dot(weighted, received.reshape(places, -1), preferred_element_type=jnp.float32)
    counts = jnp.sum(weighted.astype(jnp.float32), axis=1)
    merged = (merged_sum / jnp.maximum(counts, 1.0)[:, None]).astype(jnp.bfloat16)
    key_bias = jnp.where(counts > 0, jnp.log(jnp.maximum(counts, 1.0)), -1e30).astype(jnp.bfloat16)
    queries = jnp.dot(merged, w_query, preferred_element_type=jnp.float32).astype(jnp.bfloat16)
    query_heads = queries.reshape(merged_rows, HEADS, HEAD)
    inverse = 1.0 / math.sqrt(HEAD)

    def attend_block(carry, item):
        row_max, total, accum = carry
        key_heads, value_heads, bias = item
        scores = (
            jnp.einsum("qhd,khd->hqk", query_heads, key_heads, preferred_element_type=jnp.float32)
            * inverse
        )
        scores = scores + bias.astype(jnp.float32)[None, None, :]
        new_max = jnp.maximum(row_max, jnp.max(scores, axis=2))
        factor = jnp.exp(row_max - new_max)
        expo = jnp.exp(scores - new_max[:, :, None])
        total = total * factor + jnp.sum(expo, axis=2)
        accum = accum * factor[:, :, None] + jnp.einsum(
            "hqk,khd->hqd",
            expo.astype(jnp.bfloat16),
            value_heads,
            preferred_element_type=jnp.float32,
        )
        return ((new_max, total, accum), None)

    start_state = (
        jnp.full((HEADS, merged_rows), -jnp.inf, jnp.float32),
        jnp.zeros((HEADS, merged_rows), jnp.float32),
        jnp.zeros((HEADS, merged_rows, HEAD), jnp.float32),
    )
    own_keys = jnp.dot(merged, w_key, preferred_element_type=jnp.float32).astype(jnp.bfloat16)
    own_values = jnp.dot(merged, w_value, preferred_element_type=jnp.float32).astype(jnp.bfloat16)
    carry = start_state
    keys = lax.all_gather(own_keys, "ctx", axis=0, tiled=True)
    values = lax.all_gather(own_values, "ctx", axis=0, tiled=True)
    bias = lax.all_gather(key_bias, "ctx", axis=0, tiled=True)
    length = keys.shape[0]
    block = math.gcd(length, 1536)
    turns = length // block
    items = (
        keys.reshape(turns, block, HEADS, HEAD),
        values.reshape(turns, block, HEADS, HEAD),
        bias.reshape(turns, block),
    )
    carry, unused = lax.scan(attend_block, carry, items)
    row_max, total, accum = carry
    attended = (
        jnp.transpose(accum / total[:, :, None], (1, 0, 2))
        .reshape(merged_rows, HEADS * HEAD)
        .astype(jnp.bfloat16)
    )
    landing_rows = landing.astype(jnp.bfloat16)
    leaving = jnp.einsum(
        "mp,md->pd", landing_rows, attended, preferred_element_type=jnp.float32
    ).astype(jnp.bfloat16)
    returned = lax.all_to_all(
        leaving.reshape(shards, slots, -1), "ctx", split_axis=0, concat_axis=0, tiled=True
    )
    picked = jnp.einsum(
        "tp,pd->td", to_bucket, returned.reshape(places, -1), preferred_element_type=jnp.float32
    ).astype(jnp.bfloat16)
    mixed = jnp.dot(picked, w_out, preferred_element_type=jnp.float32).astype(jnp.bfloat16)
    return mixed


def on_device(tokens, owner, slot_map, *weights):
    tok, width = tokens.shape
    shards = lax.axis_size("ctx")
    fits = shards * tok * width * tokens.dtype.itemsize <= GATHERED_MAX
    paired = shards >= 8 and shards & (shards - 1) == 0 and shards <= LANES
    shaped = slot_map.shape[2] + 3 <= META and tok <= LANES and (shards * tok) % LANES == 0
    plan = on_device_gathered if fits and paired and shaped else on_device_exchanged
    return plan(tokens, owner, slot_map, *weights)


def solution(mesh):
    in_specs = (
        P(("groups", "ctx"), None),
        P(("groups", "ctx"), None),
        P(("groups", "ctx"), None, None),
        P(("groups", "ctx")),
        P(),
        P(),
        P(),
        P(),
    )
    out_specs = P(("groups", "ctx"), None)
    return jax.shard_map(
        on_device, mesh=mesh, in_specs=in_specs, out_specs=out_specs, check_vma=False
    )
```

```python
import functools
import math

import jax
import jax.numpy as jnp
from jax import lax
from jax.experimental import pallas as pl
from jax.experimental.pallas import tpu as pltpu
from jax.sharding import PartitionSpec as P

HEADS = 8
HEAD = 72
META = 16
LANES = 128
GATHERED_MAX = 8 << 20
VMEM_PREP = 16 << 20
VMEM_MERGE = 12 << 20
VMEM_TAIL = 20 << 20
F32 = jnp.float32
BF16 = jnp.bfloat16
NT = (((1,), (1,)), ((), ()))
TN = (((0,), (0,)), ((), ()))
NN = (((1,), (0,)), ((), ()))


def dot(a, b, dims=NN):
    return lax.dot_general(a, b, dims, preferred_element_type=F32)


def ring_index(k, core, rows):
    k = k % (2 * rows)
    row, column = (k, 0) if k < rows else (2 * rows - 1 - k, 1)
    return row * 4 + column * 2 + core


def ring_moves(shards, crossing):
    rows = shards // 4
    moves = []
    for k in range(2 * rows):
        for core, step in ((0, 1), (1, -1)):
            source = ring_index(k, core ^ crossing, rows)
            moves.append((source, ring_index(k + step, core, rows)))
    return moves


def senders(shards, me):
    rows = shards // 4
    row, column, core = me // 4, (me // 2) % 2, me % 2
    k = jnp.where(column == 0, row, 2 * rows - 1 - row)
    d = 2 * core - 1

    def at(offset, core):
        p = (k + offset + 2 * rows) % (2 * rows)
        back = p >= rows
        row = jnp.where(back, 2 * rows - 1 - p, p)
        return row * 4 + jnp.where(back, 2, 0) + core

    swapped = 1 - core
    found = [me, me ^ 1]
    for s in range(1, rows):
        found += [at(d * s, core), at(-d * s, swapped), at(d * s, swapped), at(-d * s, core)]
    found += [at(d * rows, core), at(-d * rows, swapped)]
    return found[1 : 1 + shards // 2] + [me] + found[1 + shards // 2 :]


def flip(x, shards):
    return x % 2 * (shards // 2) + x // 2 % 2 * (shards // 4) + x // 4


def meta_kernel(slots, owner_ref, sizes_ref, map_ref, out_ref):
    tok = owner_ref.shape[1]

    def wide(x):
        x = x.astype(F32)
        return jnp.concatenate([x, jnp.zeros((1, LANES - x.shape[1]), F32)], axis=1)

    row = wide(owner_ref[...])
    column = jnp.transpose(jnp.broadcast_to(row, (8, LANES)), (1, 0))[:, 0:1]
    first = lax.broadcasted_iota(jnp.int32, (LANES, LANES), 0)
    second = lax.broadcasted_iota(jnp.int32, (LANES, LANES), 1)
    earlier = (first < second) & (column == row)
    rank = jnp.sum(jnp.where(earlier, 1.0, 0.0), axis=0, keepdims=True)
    rows = [wide(map_ref[r]) for r in range(slots)] + [row, rank, wide(sizes_ref[...])]
    sub = lax.broadcasted_iota(jnp.int32, (META, LANES), 0)
    out = jnp.zeros((META, LANES), F32)
    for r, x in enumerate(rows):
        out = jnp.where(sub == r, x, out)
    out_ref[...] = out.astype(BF16)


def prep_kernel(
    shards, slots, tok, merged_rows, g_ref,
    m_ref, inv_ref, bias_ref, gf, dest_row, size_row,
):
    me = lax.axis_index("ctx")
    me_flipped = flip(me, shards)
    total = merged_rows * shards
    gf[...] = g_ref[...].astype(F32)
    by_sender = jnp.transpose(gf[...], (1, 0))[:shards].astype(BF16)
    places = shards * META
    bucket = lax.broadcasted_iota(jnp.int32, (places, LANES), 0)
    sender_iota = lax.broadcasted_iota(jnp.int32, (shards, LANES), 0)
    for j, e in enumerate(senders(shards, me)):
        base = flip(e ^ me, shards) * META
        own = gf[pl.ds(base + slots, 1), :].astype(jnp.int32)
        rank = gf[pl.ds(base + slots + 1, 1), :].astype(jnp.int32)
        size = gf[pl.ds(base + slots + 2, 1), :]
        hot = jnp.where(bucket == (flip(own, shards) ^ me_flipped) * META + rank, 1.0, 0.0).astype(BF16)
        found = dot(by_sender, hot)
        slot = jnp.sum(jnp.where(sender_iota == e, found, 0.0), axis=0, keepdims=True)
        dest = own.astype(F32) * merged_rows + slot
        dest_row[:, j * tok : (j + 1) * tok] = dest[:, :tok]
        size_row[:, j * tok : (j + 1) * tok] = size[:, :tok]
        if j == shards // 2:
            mine = dest
    mine = jnp.broadcast_to(mine, (8, LANES))
    mine = jnp.transpose(mine, (1, 0))[:tok, 0:1]
    mine = jnp.broadcast_to(mine, (tok, LANES))
    slot_of_row = lax.broadcasted_iota(jnp.int32, (total, LANES), 0).astype(F32)
    slot_of_row = jnp.concatenate([slot_of_row, mine], axis=0)
    count = jnp.zeros(slot_of_row.shape, F32)
    for b in range(shards * tok // LANES):
        cols = slice(b * LANES, (b + 1) * LANES)
        piece = jnp.where(slot_of_row == dest_row[:, cols], size_row[:, cols], 0.0)
        count = count + piece
        m_ref[:, cols] = piece.astype(BF16)
    inv_ref[...] = 1.0 / jnp.maximum(jnp.sum(count, axis=1, keepdims=True), 1.0)
    count_row = dot(jnp.ones((8, LANES), BF16), count[:total].astype(BF16), NT)[0:1]
    bias = jnp.where(count_row > 0, jnp.log(jnp.maximum(count_row, 1.0)), -1e30)
    bias_ref[...] = bias.astype(BF16).astype(F32)


def cost(flops, nbytes):
    return pl.CostEstimate(flops=flops, bytes_accessed=nbytes, transcendentals=0)


def gather_blocks(blocks, tok_s):
    tok = blocks[0].shape[0]
    for j, block in enumerate(blocks):
        tok_s[j * tok : (j + 1) * tok, :] = block[...]


def merge_kernel(n_blocks, first, *refs):
    blocks, (m_ref, *before, acc_ref, tok_s) = refs[:n_blocks], refs[n_blocks:]
    gather_blocks(blocks, tok_s)
    cols = slice(first, first + tok_s.shape[0])
    acc = dot(m_ref[:, cols], tok_s[...])
    acc_ref[...] = acc + before[0][...] if before else acc


def tail_kernel(n_blocks, first, *refs):
    blocks = refs[:n_blocks]
    (acc_ref, m_ref, inv_ref, bias_ref, wq_ref, wk_ref, wv_ref, wo_ref, out_ref,
     tok_s, merged_s, att_s) = refs[n_blocks:]
    gather_blocks(blocks, tok_s)
    acc = acc_ref[...] + dot(m_ref[:, first:], tok_s[...])
    merged_s[...] = (acc * inv_ref[...]).astype(BF16)
    total = bias_ref.shape[1]
    merged = merged_s[:total, :]
    q_t = dot(wq_ref[...], merged_s[total:, :], NT)
    k_t = dot(wk_ref[...], merged, NT)
    v_t = dot(wv_ref[...], merged, NT)
    inverse = 1.0 / math.sqrt(HEAD)
    bias = bias_ref[...]
    for h in range(HEADS):
        rows = slice(h * HEAD, (h + 1) * HEAD)
        scores = dot(q_t[rows].astype(BF16), k_t[rows].astype(BF16), TN) * inverse + bias
        top = jnp.max(scores, axis=1, keepdims=True)
        expo = jnp.exp(scores - top)
        whole = jnp.sum(expo, axis=1, keepdims=True)
        att_s[:, rows] = dot(expo.astype(BF16), v_t[rows].astype(BF16), NT) / whole
    out_ref[...] = dot(att_s[...].astype(BF16), wo_ref[...]).astype(BF16)


def on_device_gathered(tokens, owner, slot_map, sizes, w_query, w_key, w_value, w_out):
    tok, width = tokens.shape
    shards = lax.axis_size("ctx")
    slots = slot_map.shape[2]
    merged_rows = tok // 2
    total = merged_rows * shards
    vmem = pl.BlockSpec(memory_space=pltpu.VMEM)
    swap = [(i, i ^ 1) for i in range(shards)]
    along, across = ring_moves(shards, 0), ring_moves(shards, 1)

    def send(x, pairs, *after):
        if after:
            x, *_ = lax.optimization_barrier((x, *after))
        return lax.ppermute(x, "ctx", pairs)

    a, b = send(tokens, along), send(tokens, across)
    other = send(tokens, swap)
    meta = pl.pallas_call(
        functools.partial(meta_kernel, slots),
        out_shape=jax.ShapeDtypeStruct((META, LANES), BF16),
        in_specs=[vmem] * 3,
        out_specs=vmem,
    )(owner.reshape(1, tok), sizes.reshape(1, tok), jnp.transpose(slot_map, (2, 0, 1)))
    metas = [meta]
    bit = shards // 2

    def spread(*after):
        nonlocal bit
        if bit:
            pairs = [(i, i ^ bit) for i in range(shards)]
            metas.append(send(jnp.concatenate(metas, axis=0), pairs, *after))
            bit //= 2

    a1 = a
    def xor(x, d, *after):
        return send(x, [(i, i ^ d) for i in range(shards)], *after)

    row = jnp.concatenate([meta] + [xor(meta, d, *(other,)) for d in range(4, shards, 4)], axis=0)
    plane = jnp.concatenate([row, xor(row, 2)], axis=0)
    metas = [plane, xor(plane, 1)]
    blocks = [tokens, other]
    for s in range(1, shards // 4):
        blocks += [a, send(a, swap), b, send(b, swap)]
        a = send(a, along)
        if s < shards // 4 - 1:
            b = send(b, along)
    rows = total + tok
    m, inv, bias = pl.pallas_call(
        functools.partial(prep_kernel, shards, slots, tok, merged_rows),
        out_shape=(
            jax.ShapeDtypeStruct((rows, shards * tok), BF16),
            jax.ShapeDtypeStruct((rows, 1), F32),
            jax.ShapeDtypeStruct((1, total), F32),
        ),
        in_specs=[vmem],
        out_specs=(vmem,) * 3,
        scratch_shapes=[
            pltpu.VMEM((shards * META, LANES), F32),
            pltpu.VMEM((1, shards * tok), F32),
            pltpu.VMEM((1, shards * tok), F32),
        ],
        compiler_params=pltpu.CompilerParams(vmem_limit_bytes=VMEM_PREP),
        cost_estimate=cost(1000, 1000),
    )(jnp.concatenate(metas, axis=0))
    blocks = blocks[1 : 1 + shards // 2] + [tokens] + blocks[1 + shards // 2 :]
    cuts = [0, shards // 2, shards - 1, shards]
    acc = []
    for low, high in zip(cuts[:-2], cuts[1:-1]):
        n = high - low
        acc = [
            pl.pallas_call(
                functools.partial(merge_kernel, n, low * tok),
                out_shape=jax.ShapeDtypeStruct((rows, width), F32),
                in_specs=[vmem] * (n + 1 + len(acc)),
                out_specs=vmem,
                scratch_shapes=[pltpu.VMEM((n * tok, width), BF16)],
                input_output_aliases={n + 1: 0} if acc else {},
                compiler_params=pltpu.CompilerParams(vmem_limit_bytes=VMEM_MERGE),
                cost_estimate=cost(1000, 1000),
            )(*blocks[low:high], m, *acc)
        ]
        if low == 0:
            blocks += [a, send(a, swap, *acc)]
    low, high = cuts[-2:]
    n = high - low
    return pl.pallas_call(
        functools.partial(tail_kernel, n, low * tok),
        out_shape=jax.ShapeDtypeStruct((tok, width), BF16),
        in_specs=[vmem] * (n + 8),
        out_specs=vmem,
        scratch_shapes=[
            pltpu.VMEM((n * tok, width), BF16),
            pltpu.VMEM((rows, width), BF16),
            pltpu.VMEM((tok, HEADS * HEAD), F32),
        ],
        compiler_params=pltpu.CompilerParams(vmem_limit_bytes=VMEM_TAIL),
        cost_estimate=cost(4 * total * width * HEADS * HEAD, 8 * width * HEADS * HEAD),
    )(*blocks[low:high], *acc, m, inv, bias, w_query.T, w_key.T, w_value.T, w_out)


def on_device_exchanged(tokens, owner, slot_map, sizes, w_query, w_key, w_value, w_out):
    tok_rows = tokens.shape[0]
    shards = lax.axis_size("ctx")
    slots = slot_map.shape[2]
    places = shards * slots
    merged_rows = tok_rows // 2
    owners = owner[:, 0]
    order = jnp.arange(tok_rows)
    earlier = order[None, :] < order[:, None]
    ranking = jnp.sum(jnp.where(earlier & (owners[:, None] == owners[None, :]), 1, 0), axis=1)
    bucket = owners * slots + ranking
    to_bucket = (bucket[:, None] == jnp.arange(places, dtype=jnp.int32)[None, :]).astype(
        jnp.bfloat16
    )
    outgoing = jnp.einsum(
        "tp,td->pd", to_bucket, tokens, preferred_element_type=jnp.float32
    ).astype(jnp.bfloat16)
    out_weights = jnp.einsum(
        "tp,t->p", to_bucket, sizes.astype(jnp.bfloat16), preferred_element_type=jnp.float32
    ).astype(jnp.bfloat16)
    received, in_weights = (
        lax.all_to_all(
            outgoing.reshape(shards, slots, -1), "ctx", split_axis=0, concat_axis=0, tiled=True
        ),
        lax.all_to_all(
            out_weights.reshape(shards, slots), "ctx", split_axis=0, concat_axis=0, tiled=True
        ),
    )
    targets = slot_map[0].reshape(places)
    landing = targets[None, :] == jnp.arange(merged_rows, dtype=jnp.int32)[:, None]
    weighted = jnp.where(landing, in_weights.reshape(places)[None, :], 0)
    merged_sum = jnp.dot(weighted, received.reshape(places, -1), preferred_element_type=jnp.float32)
    counts = jnp.sum(weighted.astype(jnp.float32), axis=1)
    merged = (merged_sum / jnp.maximum(counts, 1.0)[:, None]).astype(jnp.bfloat16)
    key_bias = jnp.where(counts > 0, jnp.log(jnp.maximum(counts, 1.0)), -1e30).astype(jnp.bfloat16)
    queries = jnp.dot(merged, w_query, preferred_element_type=jnp.float32).astype(jnp.bfloat16)
    query_heads = queries.reshape(merged_rows, HEADS, HEAD)
    inverse = 1.0 / math.sqrt(HEAD)

    def attend_block(carry, item):
        row_max, total, accum = carry
        key_heads, value_heads, bias = item
        scores = (
            jnp.einsum("qhd,khd->hqk", query_heads, key_heads, preferred_element_type=jnp.float32)
            * inverse
        )
        scores = scores + bias.astype(jnp.float32)[None, None, :]
        new_max = jnp.maximum(row_max, jnp.max(scores, axis=2))
        factor = jnp.exp(row_max - new_max)
        expo = jnp.exp(scores - new_max[:, :, None])
        total = total * factor + jnp.sum(expo, axis=2)
        accum = accum * factor[:, :, None] + jnp.einsum(
            "hqk,khd->hqd",
            expo.astype(jnp.bfloat16),
            value_heads,
            preferred_element_type=jnp.float32,
        )
        return ((new_max, total, accum), None)

    start_state = (
        jnp.full((HEADS, merged_rows), -jnp.inf, jnp.float32),
        jnp.zeros((HEADS, merged_rows), jnp.float32),
        jnp.zeros((HEADS, merged_rows, HEAD), jnp.float32),
    )
    own_keys = jnp.dot(merged, w_key, preferred_element_type=jnp.float32).astype(jnp.bfloat16)
    own_values = jnp.dot(merged, w_value, preferred_element_type=jnp.float32).astype(jnp.bfloat16)
    carry = start_state
    keys = lax.all_gather(own_keys, "ctx", axis=0, tiled=True)
    values = lax.all_gather(own_values, "ctx", axis=0, tiled=True)
    bias = lax.all_gather(key_bias, "ctx", axis=0, tiled=True)
    length = keys.shape[0]
    block = math.gcd(length, 1536)
    turns = length // block
    items = (
        keys.reshape(turns, block, HEADS, HEAD),
        values.reshape(turns, block, HEADS, HEAD),
        bias.reshape(turns, block),
    )
    carry, unused = lax.scan(attend_block, carry, items)
    row_max, total, accum = carry
    attended = (
        jnp.transpose(accum / total[:, :, None], (1, 0, 2))
        .reshape(merged_rows, HEADS * HEAD)
        .astype(jnp.bfloat16)
    )
    landing_rows = landing.astype(jnp.bfloat16)
    leaving = jnp.einsum(
        "mp,md->pd", landing_rows, attended, preferred_element_type=jnp.float32
    ).astype(jnp.bfloat16)
    returned = lax.all_to_all(
        leaving.reshape(shards, slots, -1), "ctx", split_axis=0, concat_axis=0, tiled=True
    )
    picked = jnp.einsum(
        "tp,pd->td", to_bucket, returned.reshape(places, -1), preferred_element_type=jnp.float32
    ).astype(jnp.bfloat16)
    mixed = jnp.dot(picked, w_out, preferred_element_type=jnp.float32).astype(jnp.bfloat16)
    return mixed


def on_device(tokens, owner, slot_map, *weights):
    tok, width = tokens.shape
    shards = lax.axis_size("ctx")
    fits = shards * tok * width * tokens.dtype.itemsize <= GATHERED_MAX
    paired = shards >= 8 and shards & (shards - 1) == 0 and shards <= LANES
    shaped = slot_map.shape[2] + 3 <= META and tok <= LANES and (shards * tok) % LANES == 0
    plan = on_device_gathered if fits and paired and shaped else on_device_exchanged
    return plan(tokens, owner, slot_map, *weights)


def solution(mesh):
    in_specs = (
        P(("groups", "ctx"), None),
        P(("groups", "ctx"), None),
        P(("groups", "ctx"), None, None),
        P(("groups", "ctx")),
        P(),
        P(),
        P(),
        P(),
    )
    out_specs = P(("groups", "ctx"), None)
    return jax.shard_map(
        on_device, mesh=mesh, in_specs=in_specs, out_specs=out_specs, check_vma=False
    )
```

```python
import functools
import math

import jax
import jax.numpy as jnp
from jax import lax
from jax.experimental import pallas as pl
from jax.experimental.pallas import tpu as pltpu
from jax.sharding import PartitionSpec as P

HEADS = 8
HEAD = 72
META = 16
LANES = 128
GATHERED_MAX = 8 << 20
VMEM_PREP = 16 << 20
VMEM_MERGE = 12 << 20
VMEM_TAIL = 20 << 20
F32 = jnp.float32
BF16 = jnp.bfloat16
NT = (((1,), (1,)), ((), ()))
TN = (((0,), (0,)), ((), ()))
NN = (((1,), (0,)), ((), ()))


def dot(a, b, dims=NN):
    return lax.dot_general(a, b, dims, preferred_element_type=F32)


def ring_index(k, core, rows):
    k = k % (2 * rows)
    row, column = (k, 0) if k < rows else (2 * rows - 1 - k, 1)
    return row * 4 + column * 2 + core


def ring_moves(shards, crossing):
    rows = shards // 4
    moves = []
    for k in range(2 * rows):
        for core, step in ((0, 1), (1, -1)):
            source = ring_index(k, core ^ crossing, rows)
            moves.append((source, ring_index(k + step, core, rows)))
    return moves


def senders(shards, me):
    rows = shards // 4
    row, column, core = me // 4, (me // 2) % 2, me % 2
    k = jnp.where(column == 0, row, 2 * rows - 1 - row)
    d = 2 * core - 1

    def at(offset, core):
        p = (k + offset + 2 * rows) % (2 * rows)
        back = p >= rows
        row = jnp.where(back, 2 * rows - 1 - p, p)
        return row * 4 + jnp.where(back, 2, 0) + core

    swapped = 1 - core
    found = [me, me ^ 1]
    for s in range(1, rows):
        found += [at(d * s, core), at(-d * s, swapped), at(d * s, swapped), at(-d * s, core)]
    found += [at(d * rows, core), at(-d * rows, swapped)]
    return found[1 : 1 + shards - 6] + [me] + found[1 + shards - 6 :]


def flip(x, shards):
    return x % 2 * (shards // 2) + x // 2 % 2 * (shards // 4) + x // 4


def meta_kernel(slots, owner_ref, sizes_ref, map_ref, out_ref):
    tok = owner_ref.shape[1]

    def wide(x):
        x = x.astype(F32)
        return jnp.concatenate([x, jnp.zeros((1, LANES - x.shape[1]), F32)], axis=1)

    row = wide(owner_ref[...])
    column = jnp.transpose(jnp.broadcast_to(row, (8, LANES)), (1, 0))[:, 0:1]
    first = lax.broadcasted_iota(jnp.int32, (LANES, LANES), 0)
    second = lax.broadcasted_iota(jnp.int32, (LANES, LANES), 1)
    earlier = (first < second) & (column == row)
    rank = jnp.sum(jnp.where(earlier, 1.0, 0.0), axis=0, keepdims=True)
    rows = [wide(map_ref[r]) for r in range(slots)] + [row, rank, wide(sizes_ref[...])]
    sub = lax.broadcasted_iota(jnp.int32, (META, LANES), 0)
    out = jnp.zeros((META, LANES), F32)
    for r, x in enumerate(rows):
        out = jnp.where(sub == r, x, out)
    out_ref[...] = out.astype(BF16)


def prep_kernel(
    shards, slots, tok, merged_rows, g_ref,
    m_ref, inv_ref, bias_ref, gf, dest_row, size_row,
):
    me = lax.axis_index("ctx")
    me_flipped = flip(me, shards)
    total = merged_rows * shards
    gf[...] = g_ref[...].astype(F32)
    by_sender = jnp.transpose(gf[...], (1, 0))[:shards].astype(BF16)
    places = shards * META
    bucket = lax.broadcasted_iota(jnp.int32, (places, LANES), 0)
    sender_iota = lax.broadcasted_iota(jnp.int32, (shards, LANES), 0)
    for j, e in enumerate(senders(shards, me)):
        base = flip(e ^ me, shards) * META
        own = gf[pl.ds(base + slots, 1), :].astype(jnp.int32)
        rank = gf[pl.ds(base + slots + 1, 1), :].astype(jnp.int32)
        size = gf[pl.ds(base + slots + 2, 1), :]
        hot = jnp.where(bucket == (flip(own, shards) ^ me_flipped) * META + rank, 1.0, 0.0).astype(BF16)
        found = dot(by_sender, hot)
        slot = jnp.sum(jnp.where(sender_iota == e, found, 0.0), axis=0, keepdims=True)
        dest = own.astype(F32) * merged_rows + slot
        dest_row[:, j * tok : (j + 1) * tok] = dest[:, :tok]
        size_row[:, j * tok : (j + 1) * tok] = size[:, :tok]
        if j == shards - 6:
            mine = dest
    mine = jnp.broadcast_to(mine, (8, LANES))
    mine = jnp.transpose(mine, (1, 0))[:tok, 0:1]
    mine = jnp.broadcast_to(mine, (tok, LANES))
    slot_of_row = lax.broadcasted_iota(jnp.int32, (total, LANES), 0).astype(F32)
    slot_of_row = jnp.concatenate([slot_of_row, mine], axis=0)
    count = jnp.zeros(slot_of_row.shape, F32)
    for b in range(shards * tok // LANES):
        cols = slice(b * LANES, (b + 1) * LANES)
        piece = jnp.where(slot_of_row == dest_row[:, cols], size_row[:, cols], 0.0)
        count = count + piece
        m_ref[:, cols] = piece.astype(BF16)
    inv_ref[...] = 1.0 / jnp.maximum(jnp.sum(count, axis=1, keepdims=True), 1.0)
    count_row = dot(jnp.ones((8, LANES), BF16), count[:total].astype(BF16), NT)[0:1]
    bias = jnp.where(count_row > 0, jnp.log(jnp.maximum(count_row, 1.0)), -1e30)
    bias_ref[...] = bias.astype(BF16).astype(F32)


def cost(flops, nbytes):
    return pl.CostEstimate(flops=flops, bytes_accessed=nbytes, transcendentals=0)


def gather_blocks(blocks, tok_s):
    tok = blocks[0].shape[0]
    for j, block in enumerate(blocks):
        tok_s[j * tok : (j + 1) * tok, :] = block[...]


def merge_kernel(n_blocks, first, *refs):
    blocks, (m_ref, *before, acc_ref, tok_s) = refs[:n_blocks], refs[n_blocks:]
    gather_blocks(blocks, tok_s)
    cols = slice(first, first + tok_s.shape[0])
    acc = dot(m_ref[:, cols], tok_s[...])
    acc_ref[...] = acc + before[0][...] if before else acc


def tail_kernel(n_blocks, first, *refs):
    blocks = refs[:n_blocks]
    (acc_ref, m_ref, inv_ref, bias_ref, wq_ref, wk_ref, wv_ref, wo_ref, out_ref,
     tok_s, merged_s, att_s) = refs[n_blocks:]
    gather_blocks(blocks, tok_s)
    acc = acc_ref[...] + dot(m_ref[:, first:], tok_s[...])
    merged_s[...] = (acc * inv_ref[...]).astype(BF16)
    total = bias_ref.shape[1]
    merged = merged_s[:total, :]
    q_t = dot(wq_ref[...], merged_s[total:, :], NT)
    k_t = dot(wk_ref[...], merged, NT)
    v_t = dot(wv_ref[...], merged, NT)
    inverse = 1.0 / math.sqrt(HEAD)
    bias = bias_ref[...]
    heads = [slice(h * HEAD, (h + 1) * HEAD) for h in range(HEADS)]
    scores = [
        dot(q_t[rows].astype(BF16), k_t[rows].astype(BF16), TN) * inverse + bias for rows in heads
    ]
    weights = []
    for score in scores:
        expo = jnp.exp(score - jnp.max(score, axis=1, keepdims=True))
        weights.append((expo.astype(BF16), jnp.sum(expo, axis=1, keepdims=True)))
    for rows, (expo, whole) in zip(heads, weights):
        att_s[:, rows] = dot(expo, v_t[rows].astype(BF16), NT) / whole
    out_ref[...] = dot(att_s[...].astype(BF16), wo_ref[...]).astype(BF16)


def on_device_gathered(tokens, owner, slot_map, sizes, w_query, w_key, w_value, w_out):
    tok, width = tokens.shape
    shards = lax.axis_size("ctx")
    slots = slot_map.shape[2]
    merged_rows = tok // 2
    total = merged_rows * shards
    vmem = pl.BlockSpec(memory_space=pltpu.VMEM)
    swap = [(i, i ^ 1) for i in range(shards)]
    along, across = ring_moves(shards, 0), ring_moves(shards, 1)

    def send(x, pairs, *after):
        if after:
            x, *_ = lax.optimization_barrier((x, *after))
        return lax.ppermute(x, "ctx", pairs)

    a, b = send(tokens, along), send(tokens, across)
    other = send(tokens, swap)
    meta = pl.pallas_call(
        functools.partial(meta_kernel, slots),
        out_shape=jax.ShapeDtypeStruct((META, LANES), BF16),
        in_specs=[vmem] * 3,
        out_specs=vmem,
    )(owner.reshape(1, tok), sizes.reshape(1, tok), jnp.transpose(slot_map, (2, 0, 1)))
    metas = [meta]
    bit = shards // 2

    def spread(*after):
        nonlocal bit
        if bit:
            pairs = [(i, i ^ bit) for i in range(shards)]
            metas.append(send(jnp.concatenate(metas, axis=0), pairs, *after))
            bit //= 2

    a1 = a
    def xor(x, d, *after):
        return send(x, [(i, i ^ d) for i in range(shards)], *after)

    row = jnp.concatenate([meta] + [xor(meta, d, *(other,)) for d in range(4, shards, 4)], axis=0)
    plane = jnp.concatenate([row, xor(row, 2)], axis=0)
    metas = [plane, xor(plane, 1)]
    blocks = [tokens, other]
    for s in range(1, shards // 4):
        blocks += [a, send(a, swap), b, send(b, swap)]
        a = send(a, along)
        if s < shards // 4 - 1:
            b = send(b, along)
    rows = total + tok
    m, inv, bias = pl.pallas_call(
        functools.partial(prep_kernel, shards, slots, tok, merged_rows),
        out_shape=(
            jax.ShapeDtypeStruct((rows, shards * tok), BF16),
            jax.ShapeDtypeStruct((rows, 1), F32),
            jax.ShapeDtypeStruct((1, total), F32),
        ),
        in_specs=[vmem],
        out_specs=(vmem,) * 3,
        scratch_shapes=[
            pltpu.VMEM((shards * META, LANES), F32),
            pltpu.VMEM((1, shards * tok), F32),
            pltpu.VMEM((1, shards * tok), F32),
        ],
        compiler_params=pltpu.CompilerParams(vmem_limit_bytes=VMEM_PREP),
        cost_estimate=cost(1000, 1000),
    )(jnp.concatenate(metas, axis=0))
    blocks = blocks[1 : 1 + shards - 6] + [tokens] + blocks[1 + shards - 6 :]
    cuts = [0, shards - 6, shards - 1, shards]
    acc = []
    for low, high in zip(cuts[:-2], cuts[1:-1]):
        n = high - low
        acc = [
            pl.pallas_call(
                functools.partial(merge_kernel, n, low * tok),
                out_shape=jax.ShapeDtypeStruct((rows, width), F32),
                in_specs=[vmem] * (n + 1 + len(acc)),
                out_specs=vmem,
                scratch_shapes=[pltpu.VMEM((n * tok, width), BF16)],
                input_output_aliases={n + 1: 0} if acc else {},
                compiler_params=pltpu.CompilerParams(vmem_limit_bytes=VMEM_MERGE),
                cost_estimate=cost(1000, 1000),
            )(*blocks[low:high], m, *acc)
        ]
        if low == 0:
            blocks += [a, send(a, swap, *acc)]
    low, high = cuts[-2:]
    n = high - low
    return pl.pallas_call(
        functools.partial(tail_kernel, n, low * tok),
        out_shape=jax.ShapeDtypeStruct((tok, width), BF16),
        in_specs=[vmem] * (n + 8),
        out_specs=vmem,
        scratch_shapes=[
            pltpu.VMEM((n * tok, width), BF16),
            pltpu.VMEM((rows, width), BF16),
            pltpu.VMEM((tok, HEADS * HEAD), F32),
        ],
        compiler_params=pltpu.CompilerParams(vmem_limit_bytes=VMEM_TAIL),
        cost_estimate=cost(4 * total * width * HEADS * HEAD, 8 * width * HEADS * HEAD),
    )(*blocks[low:high], *acc, m, inv, bias, w_query.T, w_key.T, w_value.T, w_out)


def on_device_exchanged(tokens, owner, slot_map, sizes, w_query, w_key, w_value, w_out):
    tok_rows = tokens.shape[0]
    shards = lax.axis_size("ctx")
    slots = slot_map.shape[2]
    places = shards * slots
    merged_rows = tok_rows // 2
    owners = owner[:, 0]
    order = jnp.arange(tok_rows)
    earlier = order[None, :] < order[:, None]
    ranking = jnp.sum(jnp.where(earlier & (owners[:, None] == owners[None, :]), 1, 0), axis=1)
    bucket = owners * slots + ranking
    to_bucket = (bucket[:, None] == jnp.arange(places, dtype=jnp.int32)[None, :]).astype(
        jnp.bfloat16
    )
    outgoing = jnp.einsum(
        "tp,td->pd", to_bucket, tokens, preferred_element_type=jnp.float32
    ).astype(jnp.bfloat16)
    out_weights = jnp.einsum(
        "tp,t->p", to_bucket, sizes.astype(jnp.bfloat16), preferred_element_type=jnp.float32
    ).astype(jnp.bfloat16)
    received, in_weights = (
        lax.all_to_all(
            outgoing.reshape(shards, slots, -1), "ctx", split_axis=0, concat_axis=0, tiled=True
        ),
        lax.all_to_all(
            out_weights.reshape(shards, slots), "ctx", split_axis=0, concat_axis=0, tiled=True
        ),
    )
    targets = slot_map[0].reshape(places)
    landing = targets[None, :] == jnp.arange(merged_rows, dtype=jnp.int32)[:, None]
    weighted = jnp.where(landing, in_weights.reshape(places)[None, :], 0)
    merged_sum = jnp.dot(weighted, received.reshape(places, -1), preferred_element_type=jnp.float32)
    counts = jnp.sum(weighted.astype(jnp.float32), axis=1)
    merged = (merged_sum / jnp.maximum(counts, 1.0)[:, None]).astype(jnp.bfloat16)
    key_bias = jnp.where(counts > 0, jnp.log(jnp.maximum(counts, 1.0)), -1e30).astype(jnp.bfloat16)
    queries = jnp.dot(merged, w_query, preferred_element_type=jnp.float32).astype(jnp.bfloat16)
    query_heads = queries.reshape(merged_rows, HEADS, HEAD)
    inverse = 1.0 / math.sqrt(HEAD)

    def attend_block(carry, item):
        row_max, total, accum = carry
        key_heads, value_heads, bias = item
        scores = (
            jnp.einsum("qhd,khd->hqk", query_heads, key_heads, preferred_element_type=jnp.float32)
            * inverse
        )
        scores = scores + bias.astype(jnp.float32)[None, None, :]
        new_max = jnp.maximum(row_max, jnp.max(scores, axis=2))
        factor = jnp.exp(row_max - new_max)
        expo = jnp.exp(scores - new_max[:, :, None])
        total = total * factor + jnp.sum(expo, axis=2)
        accum = accum * factor[:, :, None] + jnp.einsum(
            "hqk,khd->hqd",
            expo.astype(jnp.bfloat16),
            value_heads,
            preferred_element_type=jnp.float32,
        )
        return ((new_max, total, accum), None)

    start_state = (
        jnp.full((HEADS, merged_rows), -jnp.inf, jnp.float32),
        jnp.zeros((HEADS, merged_rows), jnp.float32),
        jnp.zeros((HEADS, merged_rows, HEAD), jnp.float32),
    )
    own_keys = jnp.dot(merged, w_key, preferred_element_type=jnp.float32).astype(jnp.bfloat16)
    own_values = jnp.dot(merged, w_value, preferred_element_type=jnp.float32).astype(jnp.bfloat16)
    carry = start_state
    keys = lax.all_gather(own_keys, "ctx", axis=0, tiled=True)
    values = lax.all_gather(own_values, "ctx", axis=0, tiled=True)
    bias = lax.all_gather(key_bias, "ctx", axis=0, tiled=True)
    length = keys.shape[0]
    block = math.gcd(length, 1536)
    turns = length // block
    items = (
        keys.reshape(turns, block, HEADS, HEAD),
        values.reshape(turns, block, HEADS, HEAD),
        bias.reshape(turns, block),
    )
    carry, unused = lax.scan(attend_block, carry, items)
    row_max, total, accum = carry
    attended = (
        jnp.transpose(accum / total[:, :, None], (1, 0, 2))
        .reshape(merged_rows, HEADS * HEAD)
        .astype(jnp.bfloat16)
    )
    landing_rows = landing.astype(jnp.bfloat16)
    leaving = jnp.einsum(
        "mp,md->pd", landing_rows, attended, preferred_element_type=jnp.float32
    ).astype(jnp.bfloat16)
    returned = lax.all_to_all(
        leaving.reshape(shards, slots, -1), "ctx", split_axis=0, concat_axis=0, tiled=True
    )
    picked = jnp.einsum(
        "tp,pd->td", to_bucket, returned.reshape(places, -1), preferred_element_type=jnp.float32
    ).astype(jnp.bfloat16)
    mixed = jnp.dot(picked, w_out, preferred_element_type=jnp.float32).astype(jnp.bfloat16)
    return mixed


def on_device(tokens, owner, slot_map, *weights):
    tok, width = tokens.shape
    shards = lax.axis_size("ctx")
    fits = shards * tok * width * tokens.dtype.itemsize <= GATHERED_MAX
    paired = shards >= 8 and shards & (shards - 1) == 0 and shards <= LANES
    shaped = slot_map.shape[2] + 3 <= META and tok <= LANES and (shards * tok) % LANES == 0
    plan = on_device_gathered if fits and paired and shaped else on_device_exchanged
    return plan(tokens, owner, slot_map, *weights)


def solution(mesh):
    in_specs = (
        P(("groups", "ctx"), None),
        P(("groups", "ctx"), None),
        P(("groups", "ctx"), None, None),
        P(("groups", "ctx")),
        P(),
        P(),
        P(),
        P(),
    )
    out_specs = P(("groups", "ctx"), None)
    return jax.shard_map(
        on_device, mesh=mesh, in_specs=in_specs, out_specs=out_specs, check_vma=False
    )
```

```python
import functools
import math

import jax
import jax.numpy as jnp
from jax import lax
from jax.experimental import pallas as pl
from jax.experimental.pallas import tpu as pltpu
from jax.sharding import PartitionSpec as P

HEADS = 8
HEAD = 72
META = 16
LANES = 128
GATHERED_MAX = 8 << 20
VMEM_META = 2 << 20
VMEM_PREP = 16 << 20
VMEM_MERGE = 12 << 20
VMEM_TAIL = 20 << 20
F32 = jnp.float32
BF16 = jnp.bfloat16
NT = (((1,), (1,)), ((), ()))
TN = (((0,), (0,)), ((), ()))
NN = (((1,), (0,)), ((), ()))


def dot(a, b, dims=NN):
    return lax.dot_general(a, b, dims, preferred_element_type=F32)


def ring_index(k, core, rows):
    k = k % (2 * rows)
    row, column = (k, 0) if k < rows else (2 * rows - 1 - k, 1)
    return row * 4 + column * 2 + core


def ring_moves(shards, crossing):
    rows = shards // 4
    moves = []
    for k in range(2 * rows):
        for core, step in ((0, 1), (1, -1)):
            source = ring_index(k, core ^ crossing, rows)
            moves.append((source, ring_index(k + step, core, rows)))
    return moves


def senders(shards, me):
    rows = shards // 4
    row, column, core = me // 4, (me // 2) % 2, me % 2
    k = jnp.where(column == 0, row, 2 * rows - 1 - row)
    d = 2 * core - 1

    def at(offset, core):
        p = (k + offset + 2 * rows) % (2 * rows)
        back = p >= rows
        row = jnp.where(back, 2 * rows - 1 - p, p)
        return row * 4 + jnp.where(back, 2, 0) + core

    swapped = 1 - core
    found = [me, me ^ 1]
    for s in range(1, rows):
        found += [at(d * s, core), at(-d * s, swapped), at(d * s, swapped), at(-d * s, core)]
    found += [at(d * rows, core), at(-d * rows, swapped)]
    return found[1 : 1 + shards - 6] + [me] + found[1 + shards - 6 :]


def flip(x, shards):
    return x % 2 * (shards // 2) + x // 2 % 2 * (shards // 4) + x // 4


def meta_kernel(slots, tok, given_ref, out_ref):

    given = [given_ref[r].astype(F32) for r in range(slots + 2)]
    lane = lax.broadcasted_iota(jnp.int32, (1, LANES), 1)
    row = jnp.where(lane < tok, given[slots], -1.0)
    column = jnp.transpose(jnp.broadcast_to(row, (8, LANES)), (1, 0))[:, 0:1]
    first = lax.broadcasted_iota(jnp.int32, (LANES, LANES), 0)
    second = lax.broadcasted_iota(jnp.int32, (LANES, LANES), 1)
    earlier = (first < second) & (column == row)
    rank = jnp.sum(jnp.where(earlier, 1.0, 0.0), axis=0, keepdims=True)
    rows = given[: slots + 1] + [rank, given[slots + 1]]
    sub = lax.broadcasted_iota(jnp.int32, (META, LANES), 0)
    out = jnp.zeros((META, LANES), F32)
    for r, x in enumerate(rows):
        out = jnp.where(sub == r, x, out)
    out_ref[...] = out.astype(BF16)


def prep_kernel(
    shards, slots, tok, merged_rows, g_ref,
    m_ref, inv_ref, bias_ref, gf, dest_row, size_row,
):
    me = lax.axis_index("ctx")
    me_flipped = flip(me, shards)
    total = merged_rows * shards
    gf[...] = g_ref[...].astype(F32)
    by_sender = jnp.transpose(gf[...], (1, 0))[:shards].astype(BF16)
    places = shards * META
    bucket = lax.broadcasted_iota(jnp.int32, (places, LANES), 0)
    sender_iota = lax.broadcasted_iota(jnp.int32, (shards, LANES), 0)
    for j, e in enumerate(senders(shards, me)):
        base = flip(e ^ me, shards) * META
        own = gf[pl.ds(base + slots, 1), :].astype(jnp.int32)
        rank = gf[pl.ds(base + slots + 1, 1), :].astype(jnp.int32)
        size = gf[pl.ds(base + slots + 2, 1), :]
        hot = jnp.where(bucket == (flip(own, shards) ^ me_flipped) * META + rank, 1.0, 0.0).astype(BF16)
        found = dot(by_sender, hot)
        slot = jnp.sum(jnp.where(sender_iota == e, found, 0.0), axis=0, keepdims=True)
        dest = own.astype(F32) * merged_rows + slot
        dest_row[:, j * tok : (j + 1) * tok] = dest[:, :tok]
        size_row[:, j * tok : (j + 1) * tok] = size[:, :tok]
        if j == shards - 6:
            mine = dest
    mine = jnp.broadcast_to(mine, (8, LANES))
    mine = jnp.transpose(mine, (1, 0))[:tok, 0:1]
    mine = jnp.broadcast_to(mine, (tok, LANES))
    slot_of_row = lax.broadcasted_iota(jnp.int32, (total, LANES), 0).astype(F32)
    slot_of_row = jnp.concatenate([slot_of_row, mine], axis=0)
    count = jnp.zeros(slot_of_row.shape, F32)
    for b in range(shards * tok // LANES):
        cols = slice(b * LANES, (b + 1) * LANES)
        piece = jnp.where(slot_of_row == dest_row[:, cols], size_row[:, cols], 0.0)
        count = count + piece
        m_ref[:, cols] = piece.astype(BF16)
    inv_ref[...] = 1.0 / jnp.maximum(jnp.sum(count, axis=1, keepdims=True), 1.0)
    count_row = dot(jnp.ones((8, LANES), BF16), count[:total].astype(BF16), NT)[0:1]
    bias = jnp.where(count_row > 0, jnp.log(jnp.maximum(count_row, 1.0)), -1e30)
    bias_ref[...] = bias.astype(BF16).astype(F32)


def cost(flops, nbytes):
    return pl.CostEstimate(flops=flops, bytes_accessed=nbytes, transcendentals=0)


def gather_blocks(blocks, tok_s):
    tok = blocks[0].shape[0]
    for j, block in enumerate(blocks):
        tok_s[j * tok : (j + 1) * tok, :] = block[...]


def merge_kernel(n_blocks, first, *refs):
    blocks, (m_ref, *before, acc_ref, tok_s) = refs[:n_blocks], refs[n_blocks:]
    gather_blocks(blocks, tok_s)
    cols = slice(first, first + tok_s.shape[0])
    acc = dot(m_ref[:, cols], tok_s[...])
    acc_ref[...] = acc + before[0][...] if before else acc


def tail_kernel(n_blocks, first, *refs):
    blocks = refs[:n_blocks]
    (acc_ref, m_ref, inv_ref, bias_ref, wq_ref, wk_ref, wv_ref, wo_ref, out_ref,
     tok_s, merged_s, att_s) = refs[n_blocks:]
    gather_blocks(blocks, tok_s)
    acc = acc_ref[...] + dot(m_ref[:, first:], tok_s[...])
    merged_s[...] = (acc * inv_ref[...]).astype(BF16)
    total = bias_ref.shape[1]
    merged = merged_s[:total, :]
    q_t = dot(wq_ref[...], merged_s[total:, :], NT)
    k_t = dot(wk_ref[...], merged, NT)
    v_t = dot(wv_ref[...], merged, NT)
    inverse = 1.0 / math.sqrt(HEAD)
    bias = bias_ref[...]
    heads = [slice(h * HEAD, (h + 1) * HEAD) for h in range(HEADS)]
    scores = [
        dot(q_t[rows].astype(BF16), k_t[rows].astype(BF16), TN) * inverse + bias for rows in heads
    ]
    weights = []
    for score in scores:
        expo = jnp.exp(score - jnp.max(score, axis=1, keepdims=True))
        weights.append((expo.astype(BF16), jnp.sum(expo, axis=1, keepdims=True)))
    for rows, (expo, whole) in zip(heads, weights):
        att_s[:, rows] = dot(expo, v_t[rows].astype(BF16), NT) / whole
    out_ref[...] = dot(att_s[...].astype(BF16), wo_ref[...]).astype(BF16)


def on_device_gathered(tokens, owner, slot_map, sizes, w_query, w_key, w_value, w_out):
    tok, width = tokens.shape
    shards = lax.axis_size("ctx")
    slots = slot_map.shape[2]
    merged_rows = tok // 2
    total = merged_rows * shards
    vmem = pl.BlockSpec(memory_space=pltpu.VMEM)
    swap = [(i, i ^ 1) for i in range(shards)]
    along, across = ring_moves(shards, 0), ring_moves(shards, 1)

    def send(x, pairs, *after):
        if after:
            x, *_ = lax.optimization_barrier((x, *after))
        return lax.ppermute(x, "ctx", pairs)

    a, b = send(tokens, along), send(tokens, across)
    other = send(tokens, swap)
    given = jnp.concatenate(
        [
            jnp.pad(x, ((0, 0), (0, 0), (0, LANES - x.shape[2])))
            for x in (
                jnp.transpose(slot_map, (2, 0, 1)),
                owner.reshape(1, 1, tok),
                sizes.reshape(1, 1, tok),
            )
        ],
        axis=0,
    )
    meta = pl.pallas_call(
        functools.partial(meta_kernel, slots, tok),
        out_shape=jax.ShapeDtypeStruct((META, LANES), BF16),
        in_specs=[vmem],
        out_specs=vmem,
        compiler_params=pltpu.CompilerParams(vmem_limit_bytes=VMEM_META),
    )(given)
    metas = [meta]
    bit = shards // 2

    def spread(*after):
        nonlocal bit
        if bit:
            pairs = [(i, i ^ bit) for i in range(shards)]
            metas.append(send(jnp.concatenate(metas, axis=0), pairs, *after))
            bit //= 2

    a1 = a
    def xor(x, d, *after):
        return send(x, [(i, i ^ d) for i in range(shards)], *after)

    row = jnp.concatenate([meta] + [xor(meta, d, *(other,)) for d in range(4, shards, 4)], axis=0)
    plane = jnp.concatenate([row, xor(row, 2)], axis=0)
    metas = [plane, xor(plane, 1)]
    blocks = [tokens, other]
    for s in range(1, shards // 4):
        blocks += [a, send(a, swap), b, send(b, swap)]
        a = send(a, along)
        if s < shards // 4 - 1:
            b = send(b, along)
    rows = total + tok
    m, inv, bias = pl.pallas_call(
        functools.partial(prep_kernel, shards, slots, tok, merged_rows),
        out_shape=(
            jax.ShapeDtypeStruct((rows, shards * tok), BF16),
            jax.ShapeDtypeStruct((rows, 1), F32),
            jax.ShapeDtypeStruct((1, total), F32),
        ),
        in_specs=[vmem],
        out_specs=(vmem,) * 3,
        scratch_shapes=[
            pltpu.VMEM((shards * META, LANES), F32),
            pltpu.VMEM((1, shards * tok), F32),
            pltpu.VMEM((1, shards * tok), F32),
        ],
        compiler_params=pltpu.CompilerParams(vmem_limit_bytes=VMEM_PREP),
        cost_estimate=cost(1000, 1000),
    )(jnp.concatenate(metas, axis=0))
    blocks = blocks[1 : 1 + shards - 6] + [tokens] + blocks[1 + shards - 6 :]
    cuts = [0, shards - 6, shards - 1, shards]
    acc = []
    for low, high in zip(cuts[:-2], cuts[1:-1]):
        n = high - low
        acc = [
            pl.pallas_call(
                functools.partial(merge_kernel, n, low * tok),
                out_shape=jax.ShapeDtypeStruct((rows, width), F32),
                in_specs=[vmem] * (n + 1 + len(acc)),
                out_specs=vmem,
                scratch_shapes=[pltpu.VMEM((n * tok, width), BF16)],
                input_output_aliases={n + 1: 0} if acc else {},
                compiler_params=pltpu.CompilerParams(vmem_limit_bytes=VMEM_MERGE),
                cost_estimate=cost(1000, 1000),
            )(*blocks[low:high], m, *acc)
        ]
        if low == 0:
            blocks += [a, send(a, swap, *acc)]
    low, high = cuts[-2:]
    n = high - low
    return pl.pallas_call(
        functools.partial(tail_kernel, n, low * tok),
        out_shape=jax.ShapeDtypeStruct((tok, width), BF16),
        in_specs=[vmem] * (n + 8),
        out_specs=vmem,
        scratch_shapes=[
            pltpu.VMEM((n * tok, width), BF16),
            pltpu.VMEM((rows, width), BF16),
            pltpu.VMEM((tok, HEADS * HEAD), F32),
        ],
        compiler_params=pltpu.CompilerParams(vmem_limit_bytes=VMEM_TAIL),
        cost_estimate=cost(4 * total * width * HEADS * HEAD, 8 * width * HEADS * HEAD),
    )(*blocks[low:high], *acc, m, inv, bias, w_query.T, w_key.T, w_value.T, w_out)


def on_device_exchanged(tokens, owner, slot_map, sizes, w_query, w_key, w_value, w_out):
    tok_rows = tokens.shape[0]
    shards = lax.axis_size("ctx")
    slots = slot_map.shape[2]
    places = shards * slots
    merged_rows = tok_rows // 2
    owners = owner[:, 0]
    order = jnp.arange(tok_rows)
    earlier = order[None, :] < order[:, None]
    ranking = jnp.sum(jnp.where(earlier & (owners[:, None] == owners[None, :]), 1, 0), axis=1)
    bucket = owners * slots + ranking
    to_bucket = (bucket[:, None] == jnp.arange(places, dtype=jnp.int32)[None, :]).astype(
        jnp.bfloat16
    )
    outgoing = jnp.einsum(
        "tp,td->pd", to_bucket, tokens, preferred_element_type=jnp.float32
    ).astype(jnp.bfloat16)
    out_weights = jnp.einsum(
        "tp,t->p", to_bucket, sizes.astype(jnp.bfloat16), preferred_element_type=jnp.float32
    ).astype(jnp.bfloat16)
    received, in_weights = (
        lax.all_to_all(
            outgoing.reshape(shards, slots, -1), "ctx", split_axis=0, concat_axis=0, tiled=True
        ),
        lax.all_to_all(
            out_weights.reshape(shards, slots), "ctx", split_axis=0, concat_axis=0, tiled=True
        ),
    )
    targets = slot_map[0].reshape(places)
    landing = targets[None, :] == jnp.arange(merged_rows, dtype=jnp.int32)[:, None]
    weighted = jnp.where(landing, in_weights.reshape(places)[None, :], 0)
    merged_sum = jnp.dot(weighted, received.reshape(places, -1), preferred_element_type=jnp.float32)
    counts = jnp.sum(weighted.astype(jnp.float32), axis=1)
    merged = (merged_sum / jnp.maximum(counts, 1.0)[:, None]).astype(jnp.bfloat16)
    key_bias = jnp.where(counts > 0, jnp.log(jnp.maximum(counts, 1.0)), -1e30).astype(jnp.bfloat16)
    queries = jnp.dot(merged, w_query, preferred_element_type=jnp.float32).astype(jnp.bfloat16)
    query_heads = queries.reshape(merged_rows, HEADS, HEAD)
    inverse = 1.0 / math.sqrt(HEAD)

    def attend_block(carry, item):
        row_max, total, accum = carry
        key_heads, value_heads, bias = item
        scores = (
            jnp.einsum("qhd,khd->hqk", query_heads, key_heads, preferred_element_type=jnp.float32)
            * inverse
        )
        scores = scores + bias.astype(jnp.float32)[None, None, :]
        new_max = jnp.maximum(row_max, jnp.max(scores, axis=2))
        factor = jnp.exp(row_max - new_max)
        expo = jnp.exp(scores - new_max[:, :, None])
        total = total * factor + jnp.sum(expo, axis=2)
        accum = accum * factor[:, :, None] + jnp.einsum(
            "hqk,khd->hqd",
            expo.astype(jnp.bfloat16),
            value_heads,
            preferred_element_type=jnp.float32,
        )
        return ((new_max, total, accum), None)

    start_state = (
        jnp.full((HEADS, merged_rows), -jnp.inf, jnp.float32),
        jnp.zeros((HEADS, merged_rows), jnp.float32),
        jnp.zeros((HEADS, merged_rows, HEAD), jnp.float32),
    )
    own_keys = jnp.dot(merged, w_key, preferred_element_type=jnp.float32).astype(jnp.bfloat16)
    own_values = jnp.dot(merged, w_value, preferred_element_type=jnp.float32).astype(jnp.bfloat16)
    carry = start_state
    keys = lax.all_gather(own_keys, "ctx", axis=0, tiled=True)
    values = lax.all_gather(own_values, "ctx", axis=0, tiled=True)
    bias = lax.all_gather(key_bias, "ctx", axis=0, tiled=True)
    length = keys.shape[0]
    block = math.gcd(length, 1536)
    turns = length // block
    items = (
        keys.reshape(turns, block, HEADS, HEAD),
        values.reshape(turns, block, HEADS, HEAD),
        bias.reshape(turns, block),
    )
    carry, unused = lax.scan(attend_block, carry, items)
    row_max, total, accum = carry
    attended = (
        jnp.transpose(accum / total[:, :, None], (1, 0, 2))
        .reshape(merged_rows, HEADS * HEAD)
        .astype(jnp.bfloat16)
    )
    landing_rows = landing.astype(jnp.bfloat16)
    leaving = jnp.einsum(
        "mp,md->pd", landing_rows, attended, preferred_element_type=jnp.float32
    ).astype(jnp.bfloat16)
    returned = lax.all_to_all(
        leaving.reshape(shards, slots, -1), "ctx", split_axis=0, concat_axis=0, tiled=True
    )
    picked = jnp.einsum(
        "tp,pd->td", to_bucket, returned.reshape(places, -1), preferred_element_type=jnp.float32
    ).astype(jnp.bfloat16)
    mixed = jnp.dot(picked, w_out, preferred_element_type=jnp.float32).astype(jnp.bfloat16)
    return mixed


def on_device(tokens, owner, slot_map, *weights):
    tok, width = tokens.shape
    shards = lax.axis_size("ctx")
    fits = shards * tok * width * tokens.dtype.itemsize <= GATHERED_MAX
    paired = shards >= 8 and shards & (shards - 1) == 0 and shards <= LANES
    shaped = slot_map.shape[2] + 3 <= META and tok <= LANES and (shards * tok) % LANES == 0
    plan = on_device_gathered if fits and paired and shaped else on_device_exchanged
    return plan(tokens, owner, slot_map, *weights)


def solution(mesh):
    in_specs = (
        P(("groups", "ctx"), None),
        P(("groups", "ctx"), None),
        P(("groups", "ctx"), None, None),
        P(("groups", "ctx")),
        P(),
        P(),
        P(),
        P(),
    )
    out_specs = P(("groups", "ctx"), None)
    return jax.shard_map(
        on_device, mesh=mesh, in_specs=in_specs, out_specs=out_specs, check_vma=False
    )
```

```python
import functools
import math

import jax
import jax.numpy as jnp
from jax import lax
from jax.experimental import pallas as pl
from jax.experimental.pallas import tpu as pltpu
from jax.sharding import PartitionSpec as P

HEADS = 8
HEAD = 72
META = 16
LANES = 128
GATHERED_MAX = 8 << 20
VMEM_META = 2 << 20
VMEM_PREP = 16 << 20
VMEM_MERGE = 12 << 20
VMEM_TAIL = 20 << 20
F32 = jnp.float32
BF16 = jnp.bfloat16
NT = (((1,), (1,)), ((), ()))
TN = (((0,), (0,)), ((), ()))
NN = (((1,), (0,)), ((), ()))


def dot(a, b, dims=NN):
    return lax.dot_general(a, b, dims, preferred_element_type=F32)


def ring_index(k, core, rows):
    k = k % (2 * rows)
    row, column = (k, 0) if k < rows else (2 * rows - 1 - k, 1)
    return row * 4 + column * 2 + core


def ring_moves(shards, crossing):
    rows = shards // 4
    moves = []
    for k in range(2 * rows):
        for core, step in ((0, 1), (1, -1)):
            source = ring_index(k, core ^ crossing, rows)
            moves.append((source, ring_index(k + step, core, rows)))
    return moves


def senders(shards, me):
    rows = shards // 4
    row, column, core = me // 4, (me // 2) % 2, me % 2
    k = jnp.where(column == 0, row, 2 * rows - 1 - row)
    d = 2 * core - 1

    def at(offset, core):
        p = (k + offset + 2 * rows) % (2 * rows)
        back = p >= rows
        row = jnp.where(back, 2 * rows - 1 - p, p)
        return row * 4 + jnp.where(back, 2, 0) + core

    swapped = 1 - core
    found = [me, me ^ 1]
    for s in range(1, rows):
        found += [at(d * s, core), at(-d * s, swapped), at(d * s, swapped), at(-d * s, core)]
    found += [at(d * rows, core), at(-d * rows, swapped)]
    return found[1 : 1 + shards - 6] + [me] + found[1 + shards - 6 :]


def flip(x, shards):
    return x % 2 * (shards // 2) + x // 2 % 2 * (shards // 4) + x // 4


def meta_kernel(slots, tok, given_ref, out_ref):

    given = [given_ref[r].astype(F32) for r in range(slots + 2)]
    lane = lax.broadcasted_iota(jnp.int32, (1, LANES), 1)
    row = jnp.where(lane < tok, given[slots], -1.0)
    column = jnp.transpose(jnp.broadcast_to(row, (8, LANES)), (1, 0))[:, 0:1]
    first = lax.broadcasted_iota(jnp.int32, (LANES, LANES), 0)
    second = lax.broadcasted_iota(jnp.int32, (LANES, LANES), 1)
    earlier = (first < second) & (column == row)
    rank = jnp.sum(jnp.where(earlier, 1.0, 0.0), axis=0, keepdims=True)
    rows = given[: slots + 1] + [rank, given[slots + 1]]
    sub = lax.broadcasted_iota(jnp.int32, (META, LANES), 0)
    out = jnp.zeros((META, LANES), F32)
    for r, x in enumerate(rows):
        out = jnp.where(sub == r, x, out)
    out_ref[...] = out.astype(BF16)


def prep_kernel(
    shards, slots, tok, merged_rows, starts, g_ref,
    m_ref, inv_ref, bias_ref, gf, dest_row, size_row,
):
    me = lax.axis_index("ctx")
    me_flipped = flip(me, shards)
    total = merged_rows * shards
    gf[...] = g_ref[...].astype(F32)
    by_sender = jnp.transpose(gf[...], (1, 0))[:shards].astype(BF16)
    places = shards * META
    bucket = lax.broadcasted_iota(jnp.int32, (places, LANES), 0)
    sender_iota = lax.broadcasted_iota(jnp.int32, (shards, LANES), 0)
    dest_row[...] = jnp.full(dest_row.shape, -1.0, F32)
    size_row[...] = jnp.zeros(size_row.shape, F32)
    for j, e in enumerate(senders(shards, me)):
        base = flip(e ^ me, shards) * META
        own = gf[pl.ds(base + slots, 1), :].astype(jnp.int32)
        rank = gf[pl.ds(base + slots + 1, 1), :].astype(jnp.int32)
        size = gf[pl.ds(base + slots + 2, 1), :]
        hot = jnp.where(bucket == (flip(own, shards) ^ me_flipped) * META + rank, 1.0, 0.0).astype(BF16)
        found = dot(by_sender, hot)
        slot = jnp.sum(jnp.where(sender_iota == e, found, 0.0), axis=0, keepdims=True)
        dest = own.astype(F32) * merged_rows + slot
        dest_row[:, starts[j] : starts[j] + tok] = dest[:, :tok]
        size_row[:, starts[j] : starts[j] + tok] = size[:, :tok]
        if j == shards - 6:
            mine = dest
    mine = jnp.broadcast_to(mine, (8, LANES))
    mine = jnp.transpose(mine, (1, 0))[:tok, 0:1]
    mine = jnp.broadcast_to(mine, (tok, LANES))
    slot_of_row = lax.broadcasted_iota(jnp.int32, (total, LANES), 0).astype(F32)
    slot_of_row = jnp.concatenate([slot_of_row, mine], axis=0)
    count = jnp.zeros(slot_of_row.shape, F32)
    for b in range(m_ref.shape[1] // LANES):
        cols = slice(b * LANES, (b + 1) * LANES)
        piece = jnp.where(slot_of_row == dest_row[:, cols], size_row[:, cols], 0.0)
        count = count + piece
        m_ref[:, cols] = piece.astype(BF16)
    inv_ref[...] = 1.0 / jnp.maximum(jnp.sum(count, axis=1, keepdims=True), 1.0)
    count_row = dot(jnp.ones((8, LANES), BF16), count[:total].astype(BF16), NT)[0:1]
    bias = jnp.where(count_row > 0, jnp.log(jnp.maximum(count_row, 1.0)), -1e30)
    bias_ref[...] = bias.astype(BF16).astype(F32)


def cost(flops, nbytes):
    return pl.CostEstimate(flops=flops, bytes_accessed=nbytes, transcendentals=0)


def gather_blocks(blocks, tok_s):
    tok = blocks[0].shape[0]
    for j, block in enumerate(blocks):
        tok_s[j * tok : (j + 1) * tok, :] = block[...]


def merge_kernel(n_blocks, first, *refs):
    blocks, (m_ref, *before, acc_ref, tok_s) = refs[:n_blocks], refs[n_blocks:]
    gather_blocks(blocks, tok_s)
    cols = slice(first, first + tok_s.shape[0])
    acc = dot(m_ref[:, cols], tok_s[...])
    acc_ref[...] = acc + before[0][...] if before else acc


def tail_kernel(n_blocks, first, *refs):
    blocks = refs[:n_blocks]
    (acc_ref, m_ref, inv_ref, bias_ref, wq_ref, wk_ref, wv_ref, wo_ref, out_ref,
     tok_s, merged_s, att_s) = refs[n_blocks:]
    gather_blocks(blocks, tok_s)
    acc = acc_ref[...] + dot(m_ref[:, first : first + tok_s.shape[0]], tok_s[...])
    merged_s[...] = (acc * inv_ref[...]).astype(BF16)
    total = bias_ref.shape[1]
    merged = merged_s[:total, :]
    q_t = dot(wq_ref[...], merged_s[total:, :], NT)
    k_t = dot(wk_ref[...], merged, NT)
    v_t = dot(wv_ref[...], merged, NT)
    inverse = 1.0 / math.sqrt(HEAD)
    bias = bias_ref[...]
    heads = [slice(h * HEAD, (h + 1) * HEAD) for h in range(HEADS)]
    scores = [
        dot(q_t[rows].astype(BF16), k_t[rows].astype(BF16), TN) * inverse + bias for rows in heads
    ]
    weights = []
    for score in scores:
        expo = jnp.exp(score - jnp.max(score, axis=1, keepdims=True))
        weights.append((expo.astype(BF16), jnp.sum(expo, axis=1, keepdims=True)))
    for rows, (expo, whole) in zip(heads, weights):
        att_s[:, rows] = dot(expo, v_t[rows].astype(BF16), NT) / whole
    out_ref[...] = dot(att_s[...].astype(BF16), wo_ref[...]).astype(BF16)


def on_device_gathered(tokens, owner, slot_map, sizes, w_query, w_key, w_value, w_out):
    tok, width = tokens.shape
    shards = lax.axis_size("ctx")
    slots = slot_map.shape[2]
    merged_rows = tok // 2
    total = merged_rows * shards
    vmem = pl.BlockSpec(memory_space=pltpu.VMEM)
    swap = [(i, i ^ 1) for i in range(shards)]
    along, across = ring_moves(shards, 0), ring_moves(shards, 1)

    def send(x, pairs, *after):
        if after:
            x, *_ = lax.optimization_barrier((x, *after))
        return lax.ppermute(x, "ctx", pairs)

    a, b = send(tokens, along), send(tokens, across)
    other = send(tokens, swap)
    given = jnp.concatenate(
        [
            jnp.pad(x, ((0, 0), (0, 0), (0, LANES - x.shape[2])))
            for x in (
                jnp.transpose(slot_map, (2, 0, 1)),
                owner.reshape(1, 1, tok),
                sizes.reshape(1, 1, tok),
            )
        ],
        axis=0,
    )
    meta = pl.pallas_call(
        functools.partial(meta_kernel, slots, tok),
        out_shape=jax.ShapeDtypeStruct((META, LANES), BF16),
        in_specs=[vmem],
        out_specs=vmem,
        compiler_params=pltpu.CompilerParams(vmem_limit_bytes=VMEM_META),
    )(given)
    metas = [meta]
    bit = shards // 2

    def spread(*after):
        nonlocal bit
        if bit:
            pairs = [(i, i ^ bit) for i in range(shards)]
            metas.append(send(jnp.concatenate(metas, axis=0), pairs, *after))
            bit //= 2

    a1 = a
    def xor(x, d, *after):
        return send(x, [(i, i ^ d) for i in range(shards)], *after)

    row = jnp.concatenate([meta] + [xor(meta, d, *(other,)) for d in range(4, shards, 4)], axis=0)
    plane = jnp.concatenate([row, xor(row, 2)], axis=0)
    metas = [plane, xor(plane, 1)]
    blocks = [tokens, other]
    for s in range(1, shards // 4):
        blocks += [a, send(a, swap), b, send(b, swap)]
        a = send(a, along)
        if s < shards // 4 - 1:
            b = send(b, along)
    rows = total + tok
    cuts = [0, shards - 6, shards - 1, shards]
    starts, lanes = [], 0
    for low, high in zip(cuts[:-1], cuts[1:]):
        starts += [lanes + i * tok for i in range(high - low)]
        lanes += -(-(high - low) * tok // LANES) * LANES
    m, inv, bias = pl.pallas_call(
        functools.partial(prep_kernel, shards, slots, tok, merged_rows, tuple(starts)),
        out_shape=(
            jax.ShapeDtypeStruct((rows, lanes), BF16),
            jax.ShapeDtypeStruct((rows, 1), F32),
            jax.ShapeDtypeStruct((1, total), F32),
        ),
        in_specs=[vmem],
        out_specs=(vmem,) * 3,
        scratch_shapes=[
            pltpu.VMEM((shards * META, LANES), F32),
            pltpu.VMEM((1, lanes), F32),
            pltpu.VMEM((1, lanes), F32),
        ],
        compiler_params=pltpu.CompilerParams(vmem_limit_bytes=VMEM_PREP),
        cost_estimate=cost(1000, 1000),
    )(jnp.concatenate(metas, axis=0))
    blocks = blocks[1 : 1 + shards - 6] + [tokens] + blocks[1 + shards - 6 :]
    acc = []
    for low, high in zip(cuts[:-2], cuts[1:-1]):
        n = high - low
        acc = [
            pl.pallas_call(
                functools.partial(merge_kernel, n, starts[low]),
                out_shape=jax.ShapeDtypeStruct((rows, width), F32),
                in_specs=[vmem] * (n + 1 + len(acc)),
                out_specs=vmem,
                scratch_shapes=[pltpu.VMEM((n * tok, width), BF16)],
                input_output_aliases={n + 1: 0} if acc else {},
                compiler_params=pltpu.CompilerParams(vmem_limit_bytes=VMEM_MERGE),
                cost_estimate=cost(1000, 1000),
            )(*blocks[low:high], m, *acc)
        ]
        if low == 0:
            blocks += [a, send(a, swap, *acc)]
    low, high = cuts[-2:]
    n = high - low
    return pl.pallas_call(
        functools.partial(tail_kernel, n, starts[low]),
        out_shape=jax.ShapeDtypeStruct((tok, width), BF16),
        in_specs=[vmem] * (n + 8),
        out_specs=vmem,
        scratch_shapes=[
            pltpu.VMEM((n * tok, width), BF16),
            pltpu.VMEM((rows, width), BF16),
            pltpu.VMEM((tok, HEADS * HEAD), F32),
        ],
        compiler_params=pltpu.CompilerParams(vmem_limit_bytes=VMEM_TAIL),
        cost_estimate=cost(4 * total * width * HEADS * HEAD, 8 * width * HEADS * HEAD),
    )(*blocks[low:high], *acc, m, inv, bias, w_query.T, w_key.T, w_value.T, w_out)


def on_device_exchanged(tokens, owner, slot_map, sizes, w_query, w_key, w_value, w_out):
    tok_rows = tokens.shape[0]
    shards = lax.axis_size("ctx")
    slots = slot_map.shape[2]
    places = shards * slots
    merged_rows = tok_rows // 2
    owners = owner[:, 0]
    order = jnp.arange(tok_rows)
    earlier = order[None, :] < order[:, None]
    ranking = jnp.sum(jnp.where(earlier & (owners[:, None] == owners[None, :]), 1, 0), axis=1)
    bucket = owners * slots + ranking
    to_bucket = (bucket[:, None] == jnp.arange(places, dtype=jnp.int32)[None, :]).astype(
        jnp.bfloat16
    )
    outgoing = jnp.einsum(
        "tp,td->pd", to_bucket, tokens, preferred_element_type=jnp.float32
    ).astype(jnp.bfloat16)
    out_weights = jnp.einsum(
        "tp,t->p", to_bucket, sizes.astype(jnp.bfloat16), preferred_element_type=jnp.float32
    ).astype(jnp.bfloat16)
    received, in_weights = (
        lax.all_to_all(
            outgoing.reshape(shards, slots, -1), "ctx", split_axis=0, concat_axis=0, tiled=True
        ),
        lax.all_to_all(
            out_weights.reshape(shards, slots), "ctx", split_axis=0, concat_axis=0, tiled=True
        ),
    )
    targets = slot_map[0].reshape(places)
    landing = targets[None, :] == jnp.arange(merged_rows, dtype=jnp.int32)[:, None]
    weighted = jnp.where(landing, in_weights.reshape(places)[None, :], 0)
    merged_sum = jnp.dot(weighted, received.reshape(places, -1), preferred_element_type=jnp.float32)
    counts = jnp.sum(weighted.astype(jnp.float32), axis=1)
    merged = (merged_sum / jnp.maximum(counts, 1.0)[:, None]).astype(jnp.bfloat16)
    key_bias = jnp.where(counts > 0, jnp.log(jnp.maximum(counts, 1.0)), -1e30).astype(jnp.bfloat16)
    queries = jnp.dot(merged, w_query, preferred_element_type=jnp.float32).astype(jnp.bfloat16)
    query_heads = queries.reshape(merged_rows, HEADS, HEAD)
    inverse = 1.0 / math.sqrt(HEAD)

    def attend_block(carry, item):
        row_max, total, accum = carry
        key_heads, value_heads, bias = item
        scores = (
            jnp.einsum("qhd,khd->hqk", query_heads, key_heads, preferred_element_type=jnp.float32)
            * inverse
        )
        scores = scores + bias.astype(jnp.float32)[None, None, :]
        new_max = jnp.maximum(row_max, jnp.max(scores, axis=2))
        factor = jnp.exp(row_max - new_max)
        expo = jnp.exp(scores - new_max[:, :, None])
        total = total * factor + jnp.sum(expo, axis=2)
        accum = accum * factor[:, :, None] + jnp.einsum(
            "hqk,khd->hqd",
            expo.astype(jnp.bfloat16),
            value_heads,
            preferred_element_type=jnp.float32,
        )
        return ((new_max, total, accum), None)

    start_state = (
        jnp.full((HEADS, merged_rows), -jnp.inf, jnp.float32),
        jnp.zeros((HEADS, merged_rows), jnp.float32),
        jnp.zeros((HEADS, merged_rows, HEAD), jnp.float32),
    )
    own_keys = jnp.dot(merged, w_key, preferred_element_type=jnp.float32).astype(jnp.bfloat16)
    own_values = jnp.dot(merged, w_value, preferred_element_type=jnp.float32).astype(jnp.bfloat16)
    carry = start_state
    keys = lax.all_gather(own_keys, "ctx", axis=0, tiled=True)
    values = lax.all_gather(own_values, "ctx", axis=0, tiled=True)
    bias = lax.all_gather(key_bias, "ctx", axis=0, tiled=True)
    length = keys.shape[0]
    block = math.gcd(length, 1536)
    turns = length // block
    items = (
        keys.reshape(turns, block, HEADS, HEAD),
        values.reshape(turns, block, HEADS, HEAD),
        bias.reshape(turns, block),
    )
    carry, unused = lax.scan(attend_block, carry, items)
    row_max, total, accum = carry
    attended = (
        jnp.transpose(accum / total[:, :, None], (1, 0, 2))
        .reshape(merged_rows, HEADS * HEAD)
        .astype(jnp.bfloat16)
    )
    landing_rows = landing.astype(jnp.bfloat16)
    leaving = jnp.einsum(
        "mp,md->pd", landing_rows, attended, preferred_element_type=jnp.float32
    ).astype(jnp.bfloat16)
    returned = lax.all_to_all(
        leaving.reshape(shards, slots, -1), "ctx", split_axis=0, concat_axis=0, tiled=True
    )
    picked = jnp.einsum(
        "tp,pd->td", to_bucket, returned.reshape(places, -1), preferred_element_type=jnp.float32
    ).astype(jnp.bfloat16)
    mixed = jnp.dot(picked, w_out, preferred_element_type=jnp.float32).astype(jnp.bfloat16)
    return mixed


def on_device(tokens, owner, slot_map, *weights):
    tok, width = tokens.shape
    shards = lax.axis_size("ctx")
    fits = shards * tok * width * tokens.dtype.itemsize <= GATHERED_MAX
    paired = shards >= 8 and shards & (shards - 1) == 0 and shards <= LANES
    shaped = slot_map.shape[2] + 3 <= META and tok <= LANES and (shards * tok) % LANES == 0
    plan = on_device_gathered if fits and paired and shaped else on_device_exchanged
    return plan(tokens, owner, slot_map, *weights)


def solution(mesh):
    in_specs = (
        P(("groups", "ctx"), None),
        P(("groups", "ctx"), None),
        P(("groups", "ctx"), None, None),
        P(("groups", "ctx")),
        P(),
        P(),
        P(),
        P(),
    )
    out_specs = P(("groups", "ctx"), None)
    return jax.shard_map(
        on_device, mesh=mesh, in_specs=in_specs, out_specs=out_specs, check_vma=False
    )
```

```python
import functools
import math

import jax
import jax.numpy as jnp
from jax import lax
from jax.experimental import pallas as pl
from jax.experimental.pallas import tpu as pltpu
from jax.sharding import PartitionSpec as P

HEADS = 8
HEAD = 72
META = 16
LANES = 128
GATHERED_MAX = 8 << 20
VMEM_META = 2 << 20
VMEM_PREP = 16 << 20
VMEM_MERGE = 12 << 20
VMEM_TAIL = 20 << 20
F32 = jnp.float32
BF16 = jnp.bfloat16
NT = (((1,), (1,)), ((), ()))
TN = (((0,), (0,)), ((), ()))
NN = (((1,), (0,)), ((), ()))


def dot(a, b, dims=NN):
    return lax.dot_general(a, b, dims, preferred_element_type=F32)


def ring_index(k, core, rows):
    k = k % (2 * rows)
    row, column = (k, 0) if k < rows else (2 * rows - 1 - k, 1)
    return row * 4 + column * 2 + core


def ring_moves(shards, crossing):
    rows = shards // 4
    moves = []
    for k in range(2 * rows):
        for core, step in ((0, 1), (1, -1)):
            source = ring_index(k, core ^ crossing, rows)
            moves.append((source, ring_index(k + step, core, rows)))
    return moves


def senders(shards, me):
    rows = shards // 4
    row, column, core = me // 4, (me // 2) % 2, me % 2
    k = jnp.where(column == 0, row, 2 * rows - 1 - row)
    d = 2 * core - 1

    def at(offset, core):
        p = (k + offset + 2 * rows) % (2 * rows)
        back = p >= rows
        row = jnp.where(back, 2 * rows - 1 - p, p)
        return row * 4 + jnp.where(back, 2, 0) + core

    swapped = 1 - core
    found = [me, me ^ 1]
    for s in range(1, rows):
        found += [at(d * s, core), at(-d * s, swapped), at(d * s, swapped), at(-d * s, core)]
    found += [at(d * rows, core), at(-d * rows, swapped)]
    return found[1 : 1 + shards - 6] + [me] + found[1 + shards - 6 :]


def flip(x, shards):
    return x % 2 * (shards // 2) + x // 2 % 2 * (shards // 4) + x // 4


def meta_kernel(slots, tok, given_ref, out_ref):

    given = [given_ref[r].astype(F32) for r in range(slots + 2)]
    lane = lax.broadcasted_iota(jnp.int32, (1, LANES), 1)
    row = jnp.where(lane < tok, given[slots], -1.0)
    column = jnp.transpose(jnp.broadcast_to(row, (8, LANES)), (1, 0))[:, 0:1]
    first = lax.broadcasted_iota(jnp.int32, (LANES, LANES), 0)
    second = lax.broadcasted_iota(jnp.int32, (LANES, LANES), 1)
    earlier = (first < second) & (column == row)
    rank = jnp.sum(jnp.where(earlier, 1.0, 0.0), axis=0, keepdims=True)
    rows = given[: slots + 1] + [rank, given[slots + 1]]
    sub = lax.broadcasted_iota(jnp.int32, (META, LANES), 0)
    out = jnp.zeros((META, LANES), F32)
    for r, x in enumerate(rows):
        out = jnp.where(sub == r, x, out)
    out_ref[...] = out.astype(BF16)


def prep_kernel(
    shards, slots, tok, merged_rows, starts, g_ref,
    m_ref, inv_ref, bias_ref, gf, dest_row, size_row,
):
    me = lax.axis_index("ctx")
    me_flipped = flip(me, shards)
    total = merged_rows * shards
    gf[...] = g_ref[...].astype(F32)
    by_sender = jnp.transpose(gf[...], (1, 0))[:shards].astype(BF16)
    places = shards * META
    bucket = lax.broadcasted_iota(jnp.int32, (places, LANES), 0)
    sender_iota = lax.broadcasted_iota(jnp.int32, (shards, LANES), 0)
    dest_row[...] = jnp.full(dest_row.shape, -1.0, F32)
    size_row[...] = jnp.zeros(size_row.shape, F32)
    for j, e in enumerate(senders(shards, me)):
        base = flip(e ^ me, shards) * META
        own = gf[pl.ds(base + slots, 1), :].astype(jnp.int32)
        rank = gf[pl.ds(base + slots + 1, 1), :].astype(jnp.int32)
        size = gf[pl.ds(base + slots + 2, 1), :]
        hot = jnp.where(bucket == (flip(own, shards) ^ me_flipped) * META + rank, 1.0, 0.0).astype(BF16)
        found = dot(by_sender, hot)
        slot = jnp.sum(jnp.where(sender_iota == e, found, 0.0), axis=0, keepdims=True)
        dest = own.astype(F32) * merged_rows + slot
        dest_row[:, starts[j] : starts[j] + tok] = dest[:, :tok]
        size_row[:, starts[j] : starts[j] + tok] = size[:, :tok]
        if j == shards - 6:
            mine = dest
    mine = jnp.broadcast_to(mine, (8, LANES))
    mine = jnp.transpose(mine, (1, 0))[:tok, 0:1]
    mine = jnp.broadcast_to(mine, (tok, LANES))
    slot_of_row = lax.broadcasted_iota(jnp.int32, (total, LANES), 0).astype(F32)
    slot_of_row = jnp.concatenate([slot_of_row, mine], axis=0)
    count = jnp.zeros(slot_of_row.shape, F32)
    for b in range(m_ref.shape[1] // LANES):
        cols = slice(b * LANES, (b + 1) * LANES)
        piece = jnp.where(slot_of_row == dest_row[:, cols], size_row[:, cols], 0.0)
        count = count + piece
        m_ref[:, cols] = piece.astype(BF16)
    inv_ref[...] = 1.0 / jnp.maximum(jnp.sum(count, axis=1, keepdims=True), 1.0)
    count_row = dot(jnp.ones((8, LANES), BF16), count[:total].astype(BF16), NT)[0:1]
    bias = jnp.where(count_row > 0, jnp.log(jnp.maximum(count_row, 1.0)), -1e30)
    bias_ref[...] = bias.astype(BF16).astype(F32)


def cost(flops, nbytes):
    return pl.CostEstimate(flops=flops, bytes_accessed=nbytes, transcendentals=0)


def gather_blocks(blocks, tok_s):
    tok = blocks[0].shape[0]
    for j, block in enumerate(blocks):
        tok_s[j * tok : (j + 1) * tok, :] = block[...]


def merge_kernel(n_blocks, first, *refs):
    blocks, (m_ref, *before, acc_ref, tok_s) = refs[:n_blocks], refs[n_blocks:]
    gather_blocks(blocks, tok_s)
    cols = slice(first, first + tok_s.shape[0])
    acc = dot(m_ref[:, cols], tok_s[...])
    acc_ref[...] = acc + before[0][...] if before else acc


def tail_kernel(n_blocks, first, *refs):
    blocks = refs[:n_blocks]
    (acc_ref, m_ref, inv_ref, bias_ref, wq_ref, wk_ref, wv_ref, wo_ref, out_ref,
     tok_s, merged_s, att_s) = refs[n_blocks:]
    gather_blocks(blocks, tok_s)
    acc = acc_ref[...] + dot(m_ref[:, first : first + tok_s.shape[0]], tok_s[...])
    merged_s[...] = (acc * inv_ref[...]).astype(BF16)
    total = bias_ref.shape[1]
    merged = merged_s[:total, :]
    q_t = dot(wq_ref[...], merged_s[total:, :], NT)
    k_t = dot(wk_ref[...], merged, NT)
    v_t = dot(wv_ref[...], merged, NT)
    inverse = 1.0 / math.sqrt(HEAD)
    bias = bias_ref[...]
    heads = [slice(h * HEAD, (h + 1) * HEAD) for h in range(HEADS)]
    scores = [
        dot(q_t[rows].astype(BF16), k_t[rows].astype(BF16), TN) * inverse + bias for rows in heads
    ]
    weights = []
    for score in scores:
        expo = jnp.exp(score - jnp.max(score, axis=1, keepdims=True))
        weights.append((expo.astype(BF16), jnp.sum(expo, axis=1, keepdims=True)))
    for rows, (expo, whole) in zip(heads, weights):
        att_s[:, rows] = dot(expo, v_t[rows].astype(BF16), NT) / whole
    out_ref[...] = dot(att_s[...].astype(BF16), wo_ref[...]).astype(BF16)


def on_device_gathered(tokens, owner, slot_map, sizes, w_query, w_key, w_value, w_out):
    tok, width = tokens.shape
    shards = lax.axis_size("ctx")
    slots = slot_map.shape[2]
    merged_rows = tok // 2
    total = merged_rows * shards
    vmem = pl.BlockSpec(memory_space=pltpu.VMEM)
    swap = [(i, i ^ 1) for i in range(shards)]
    along, across = ring_moves(shards, 0), ring_moves(shards, 1)

    def send(x, pairs, *after):
        if after:
            x, *_ = lax.optimization_barrier((x, *after))
        return lax.ppermute(x, "ctx", pairs)

    a, b = send(tokens, along), send(tokens, across)
    other = send(tokens, swap)
    given = jnp.concatenate(
        [
            jnp.pad(x, ((0, 0), (0, 0), (0, LANES - x.shape[2])))
            for x in (
                jnp.transpose(slot_map, (2, 0, 1)),
                owner.reshape(1, 1, tok),
                sizes.reshape(1, 1, tok),
            )
        ],
        axis=0,
    )
    meta = pl.pallas_call(
        functools.partial(meta_kernel, slots, tok),
        out_shape=jax.ShapeDtypeStruct((META, LANES), BF16),
        in_specs=[vmem],
        out_specs=vmem,
        compiler_params=pltpu.CompilerParams(vmem_limit_bytes=VMEM_META),
    )(given)
    metas = [meta]
    bit = shards // 2

    def spread(*after):
        nonlocal bit
        if bit:
            pairs = [(i, i ^ bit) for i in range(shards)]
            metas.append(send(jnp.concatenate(metas, axis=0), pairs, *after))
            bit //= 2

    a1 = a
    def xor(x, d, *after):
        return send(x, [(i, i ^ d) for i in range(shards)], *after)

    row = jnp.concatenate([meta] + [xor(meta, d, *(other,)) for d in range(4, shards, 4)], axis=0)
    plane = jnp.concatenate([row, xor(row, 2)], axis=0)
    metas = [plane, xor(plane, 1)]
    blocks = [tokens, other]
    for s in range(1, shards // 4):
        blocks += [a, send(a, swap), b, send(b, swap)]
        a = send(a, along)
        if s < shards // 4 - 1:
            b = send(b, along)
    rows = total + tok
    cuts = [0, shards - 6, shards - 4, shards]
    starts, lanes = [], 0
    for low, high in zip(cuts[:-1], cuts[1:]):
        starts += [lanes + i * tok for i in range(high - low)]
        lanes += -(-(high - low) * tok // LANES) * LANES
    m, inv, bias = pl.pallas_call(
        functools.partial(prep_kernel, shards, slots, tok, merged_rows, tuple(starts)),
        out_shape=(
            jax.ShapeDtypeStruct((rows, lanes), BF16),
            jax.ShapeDtypeStruct((rows, 1), F32),
            jax.ShapeDtypeStruct((1, total), F32),
        ),
        in_specs=[vmem],
        out_specs=(vmem,) * 3,
        scratch_shapes=[
            pltpu.VMEM((shards * META, LANES), F32),
            pltpu.VMEM((1, lanes), F32),
            pltpu.VMEM((1, lanes), F32),
        ],
        compiler_params=pltpu.CompilerParams(vmem_limit_bytes=VMEM_PREP),
        cost_estimate=cost(1000, 1000),
    )(jnp.concatenate(metas, axis=0))
    blocks = blocks[1 : 1 + shards - 6] + [tokens] + blocks[1 + shards - 6 :]
    acc = []
    for low, high in zip(cuts[:-2], cuts[1:-1]):
        n = high - low
        acc = [
            pl.pallas_call(
                functools.partial(merge_kernel, n, starts[low]),
                out_shape=jax.ShapeDtypeStruct((rows, width), F32),
                in_specs=[vmem] * (n + 1 + len(acc)),
                out_specs=vmem,
                scratch_shapes=[pltpu.VMEM((n * tok, width), BF16)],
                input_output_aliases={n + 1: 0} if acc else {},
                compiler_params=pltpu.CompilerParams(vmem_limit_bytes=VMEM_MERGE),
                cost_estimate=cost(1000, 1000),
            )(*blocks[low:high], m, *acc)
        ]
        if low == 0:
            blocks += [a, send(a, swap, *acc)]
    low, high = cuts[-2:]
    n = high - low
    return pl.pallas_call(
        functools.partial(tail_kernel, n, starts[low]),
        out_shape=jax.ShapeDtypeStruct((tok, width), BF16),
        in_specs=[vmem] * (n + 8),
        out_specs=vmem,
        scratch_shapes=[
            pltpu.VMEM((n * tok, width), BF16),
            pltpu.VMEM((rows, width), BF16),
            pltpu.VMEM((tok, HEADS * HEAD), F32),
        ],
        compiler_params=pltpu.CompilerParams(vmem_limit_bytes=VMEM_TAIL),
        cost_estimate=cost(4 * total * width * HEADS * HEAD, 8 * width * HEADS * HEAD),
    )(*blocks[low:high], *acc, m, inv, bias, w_query.T, w_key.T, w_value.T, w_out)


def on_device_exchanged(tokens, owner, slot_map, sizes, w_query, w_key, w_value, w_out):
    tok_rows = tokens.shape[0]
    shards = lax.axis_size("ctx")
    slots = slot_map.shape[2]
    places = shards * slots
    merged_rows = tok_rows // 2
    owners = owner[:, 0]
    order = jnp.arange(tok_rows)
    earlier = order[None, :] < order[:, None]
    ranking = jnp.sum(jnp.where(earlier & (owners[:, None] == owners[None, :]), 1, 0), axis=1)
    bucket = owners * slots + ranking
    to_bucket = (bucket[:, None] == jnp.arange(places, dtype=jnp.int32)[None, :]).astype(
        jnp.bfloat16
    )
    outgoing = jnp.einsum(
        "tp,td->pd", to_bucket, tokens, preferred_element_type=jnp.float32
    ).astype(jnp.bfloat16)
    out_weights = jnp.einsum(
        "tp,t->p", to_bucket, sizes.astype(jnp.bfloat16), preferred_element_type=jnp.float32
    ).astype(jnp.bfloat16)
    received, in_weights = (
        lax.all_to_all(
            outgoing.reshape(shards, slots, -1), "ctx", split_axis=0, concat_axis=0, tiled=True
        ),
        lax.all_to_all(
            out_weights.reshape(shards, slots), "ctx", split_axis=0, concat_axis=0, tiled=True
        ),
    )
    targets = slot_map[0].reshape(places)
    landing = targets[None, :] == jnp.arange(merged_rows, dtype=jnp.int32)[:, None]
    weighted = jnp.where(landing, in_weights.reshape(places)[None, :], 0)
    merged_sum = jnp.dot(weighted, received.reshape(places, -1), preferred_element_type=jnp.float32)
    counts = jnp.sum(weighted.astype(jnp.float32), axis=1)
    merged = (merged_sum / jnp.maximum(counts, 1.0)[:, None]).astype(jnp.bfloat16)
    key_bias = jnp.where(counts > 0, jnp.log(jnp.maximum(counts, 1.0)), -1e30).astype(jnp.bfloat16)
    queries = jnp.dot(merged, w_query, preferred_element_type=jnp.float32).astype(jnp.bfloat16)
    query_heads = queries.reshape(merged_rows, HEADS, HEAD)
    inverse = 1.0 / math.sqrt(HEAD)

    def attend_block(carry, item):
        row_max, total, accum = carry
        key_heads, value_heads, bias = item
        scores = (
            jnp.einsum("qhd,khd->hqk", query_heads, key_heads, preferred_element_type=jnp.float32)
            * inverse
        )
        scores = scores + bias.astype(jnp.float32)[None, None, :]
        new_max = jnp.maximum(row_max, jnp.max(scores, axis=2))
        factor = jnp.exp(row_max - new_max)
        expo = jnp.exp(scores - new_max[:, :, None])
        total = total * factor + jnp.sum(expo, axis=2)
        accum = accum * factor[:, :, None] + jnp.einsum(
            "hqk,khd->hqd",
            expo.astype(jnp.bfloat16),
            value_heads,
            preferred_element_type=jnp.float32,
        )
        return ((new_max, total, accum), None)

    start_state = (
        jnp.full((HEADS, merged_rows), -jnp.inf, jnp.float32),
        jnp.zeros((HEADS, merged_rows), jnp.float32),
        jnp.zeros((HEADS, merged_rows, HEAD), jnp.float32),
    )
    own_keys = jnp.dot(merged, w_key, preferred_element_type=jnp.float32).astype(jnp.bfloat16)
    own_values = jnp.dot(merged, w_value, preferred_element_type=jnp.float32).astype(jnp.bfloat16)
    carry = start_state
    keys = lax.all_gather(own_keys, "ctx", axis=0, tiled=True)
    values = lax.all_gather(own_values, "ctx", axis=0, tiled=True)
    bias = lax.all_gather(key_bias, "ctx", axis=0, tiled=True)
    length = keys.shape[0]
    block = math.gcd(length, 1536)
    turns = length // block
    items = (
        keys.reshape(turns, block, HEADS, HEAD),
        values.reshape(turns, block, HEADS, HEAD),
        bias.reshape(turns, block),
    )
    carry, unused = lax.scan(attend_block, carry, items)
    row_max, total, accum = carry
    attended = (
        jnp.transpose(accum / total[:, :, None], (1, 0, 2))
        .reshape(merged_rows, HEADS * HEAD)
        .astype(jnp.bfloat16)
    )
    landing_rows = landing.astype(jnp.bfloat16)
    leaving = jnp.einsum(
        "mp,md->pd", landing_rows, attended, preferred_element_type=jnp.float32
    ).astype(jnp.bfloat16)
    returned = lax.all_to_all(
        leaving.reshape(shards, slots, -1), "ctx", split_axis=0, concat_axis=0, tiled=True
    )
    picked = jnp.einsum(
        "tp,pd->td", to_bucket, returned.reshape(places, -1), preferred_element_type=jnp.float32
    ).astype(jnp.bfloat16)
    mixed = jnp.dot(picked, w_out, preferred_element_type=jnp.float32).astype(jnp.bfloat16)
    return mixed


def on_device(tokens, owner, slot_map, *weights):
    tok, width = tokens.shape
    shards = lax.axis_size("ctx")
    fits = shards * tok * width * tokens.dtype.itemsize <= GATHERED_MAX
    paired = shards >= 8 and shards & (shards - 1) == 0 and shards <= LANES
    shaped = slot_map.shape[2] + 3 <= META and tok <= LANES and (shards * tok) % LANES == 0
    plan = on_device_gathered if fits and paired and shaped else on_device_exchanged
    return plan(tokens, owner, slot_map, *weights)


def solution(mesh):
    in_specs = (
        P(("groups", "ctx"), None),
        P(("groups", "ctx"), None),
        P(("groups", "ctx"), None, None),
        P(("groups", "ctx")),
        P(),
        P(),
        P(),
        P(),
    )
    out_specs = P(("groups", "ctx"), None)
    return jax.shard_map(
        on_device, mesh=mesh, in_specs=in_specs, out_specs=out_specs, check_vma=False
    )
```
